768 devices in a mesh: gx: 48 (over z, x), gy: 16 (over y, core).
Axes of the slice: x: 4, y: 8, z: 12, core: 2. Of those that a mesh axis runs over, the one named last changes fastest.
Arguments:
- rhs: float32 [384, 1536, 64], P('gx', 'gy'), may hold values from -6 to 6
- active: int32 [384, 1536], P('gx', 'gy'), may hold values 0 or 1
- fine_types: int32 [5, 384, 1536], P(None, 'gx', 'gy'), may hold values from 0 to 3
- fine_scales: float32 [5, 384, 1536], P(None, 'gx', 'gy'), may hold values from 0.5 to 2
- fine_table: float32 [5, 4, 64, 64], replicated, may hold values from -0.9 to 2.6
- fine_smoother: float32 [4, 64, 64], replicated, may hold values from -0.15 to 0.65
- fine_groups: int32 [384, 1536], P('gx', 'gy'), may hold values from 0 to 191
- coarse_types: int32 [5, 192, 768], P(None, 'gx', 'gy'), may hold values from 0 to 3
- coarse_scales: float32 [5, 192, 768], P(None, 'gx', 'gy'), may hold values from 0.5 to 2
- coarse_table: float32 [5, 4, 64, 64], replicated, may hold values from -3.6 to 10.4
- coarse_smoother: float32 [4, 64, 64], replicated, may hold values from -0.04 to 0.165
- coarse_groups: int32 [192, 768], P('gx', 'gy'), may hold values from 0 to 1
- coarsest: float32 [48, 2048, 2048], P('gx', 'gy'), as said below
Outputs:
- solution: float32 [384, 1536, 64], P('gx', 'gy')
- residual: float32 [384, 1536, 64], P('gx', 'gy')
The draws below stay inside these ranges and needn't reach their ends.
Inputs may be any that keep to these rules, and one draw needn't show every extreme that they name: `coarsest`: each subgroup's matrix is symmetric. `fine_groups`: numbered row-major within the same device's tile of 4 x 48 second-level rows. `coarse_groups`: numbered within the same device's 2 third-level rows.
All inputs are finite; a program needn't handle non-finite values. No bound on the sum of `active` on one device may be relied on, other than what follows from the above.
Results may differ from the reference program's by a relative error of at most 0.00016.
Values sent between devices are 32-bit elements; how exact they have to be, the bound alone decides.
A program may use at most 64 MiB of HBM per device.

```python
import math
import jax
import jax.numpy as jnp
from jax import lax

BLOCK = 64
KINDS = 4
GROUPS = 2
TILE_X = 8
TILE_Y = 96
COARSE_X = 4
COARSE_Y = 48
NX = 384
NY = 1536
NXC = 192
NYC = 768
LEVEL_ROWS = 2048
N_GX = 48
N_GY = 16


def block_draw(key, lead_shape, centres, spread):
    noise = jnp.clip(jax.random.normal(key, lead_shape + (BLOCK, BLOCK), jnp.float32), -4.0, 4.0)
    noise = noise * (spread / math.sqrt(BLOCK))
    return centres * jnp.eye(BLOCK, dtype=jnp.float32) + noise


def draw_fine_table(key, part):
    key = jax.random.fold_in(key, 1)
    centres = jnp.array([2.0, -0.3, -0.3, -0.3, -0.3], jnp.float32).reshape(5, 1, 1, 1)
    return block_draw(key, (5, KINDS), centres, 0.6)


def draw_coarse_table(key, part):
    key = jax.random.fold_in(key, 2)
    centres = jnp.array([8.0, -1.2, -1.2, -1.2, -1.2], jnp.float32).reshape(5, 1, 1, 1)
    return block_draw(key, (5, KINDS), centres, 2.4)


def draw_fine_smoother(key, part):
    key = jax.random.fold_in(key, 3)
    return block_draw(key, (KINDS,), 0.5, 0.15)


def draw_coarse_smoother(key, part):
    key = jax.random.fold_in(key, 4)
    return block_draw(key, (KINDS,), 0.125, 0.04)


def draw_coarsest(key, part):
    key = jax.random.fold_in(key, 5)
    noise = jnp.clip(jax.random.normal(key, (N_GX, LEVEL_ROWS, LEVEL_ROWS), jnp.float32), -4.0, 4.0)
    noise = noise * (0.5 / math.sqrt(LEVEL_ROWS))
    paired = (noise + jnp.swapaxes(noise, 1, 2)) * 0.5
    factor = GROUPS / (COARSE_X * COARSE_Y)
    return (jnp.eye(LEVEL_ROWS, dtype=jnp.float32) + paired) * factor


def place_ends(values, rng, smallest, high):
    extent = values.shape
    index_at = [jax.random.randint(jax.random.fold_in(rng, axis), (), 0, extent[axis]) for axis in range(len(extent))]
    values = values.at[tuple(index_at)].set(smallest)
    longest = extent.index(max(extent))
    index_at[longest] = (index_at[longest] + 1) % extent[longest]
    return values.at[tuple(index_at)].set(high)


def level_of(own_key, extent, split, low, top_value):
    def one(position, blocks):
        draws = jax.random.uniform(jax.random.fold_in(jax.random.fold_in(own_key, 6), position), (blocks,), jnp.float32, low / len(split), top_value / len(split))
        return jnp.repeat(jnp.exp(draws), extent[position] // blocks).reshape((-1,) + (1,) * (len(extent) - position - 1))

    gain = one(*split[0])
    for cut in split[1:]:
        gain = gain * one(*cut)
    return gain


def scatter_about(rng, shape, scale, most, split=(), held_as=jnp.bfloat16):
    result = scale * jax.random.normal(rng, shape, jnp.float32)
    if split:
        result = result * level_of(rng, shape, split, -0.22, 0.18)
    return jnp.clip(result, -most, most).astype(held_as)


def setup_inputs(seed: int = 0) -> dict:
    splits = jax.random.split(jax.random.key(seed), 14)
    return {
        "rhs": scatter_about(splits[0], (NX, NY, BLOCK), 1.0, 6.0, ((0, 48), (1, 16)), jnp.float32),
        "active": place_ends((jax.random.randint(splits[1], (NX, NY), 0, 8) < 7).astype(jnp.int32), jax.random.fold_in(splits[1], 1), 0, 1),
        "fine_types": place_ends(jax.random.randint(splits[2], (5, NX, NY), 0, KINDS), jax.random.fold_in(splits[2], 1), 0, KINDS - 1).astype(jnp.int32),
        "fine_scales": jnp.clip(jnp.exp(math.log(2.0) - 1.3862944 * jax.random.uniform(splits[3], (5, NX, NY), jnp.float32) ** level_of(splits[3], (5, NX, NY), ((1, 48), (2, 16)), -0.2, 0.2)), 0.5, 2.0),
        "fine_table": draw_fine_table(jax.random.fold_in(splits[13], 71), 0),
        "fine_smoother": draw_fine_smoother(jax.random.fold_in(splits[13], 71), 0),
        "fine_groups": place_ends(jax.random.randint(splits[6], (NX, NY), 0, COARSE_X * COARSE_Y), jax.random.fold_in(splits[6], 1), 0, (COARSE_X * COARSE_Y) - 1).astype(jnp.int32),
        "coarse_types": place_ends(jax.random.randint(splits[7], (5, NXC, NYC), 0, KINDS), jax.random.fold_in(splits[7], 1), 0, KINDS - 1).astype(jnp.int32),
        "coarse_scales": jnp.clip(jnp.exp(math.log(2.0) - 1.3862944 * jax.random.uniform(splits[8], (5, NXC, NYC), jnp.float32) ** level_of(splits[8], (5, NXC, NYC), ((1, 48), (2, 16)), -0.2, 0.2)), 0.5, 2.0),
        "coarse_table": draw_coarse_table(jax.random.fold_in(splits[13], 71), 0),
        "coarse_smoother": draw_coarse_smoother(jax.random.fold_in(splits[13], 71), 0),
        "coarse_groups": place_ends(jax.random.randint(splits[11], (NXC, NYC), 0, GROUPS), jax.random.fold_in(splits[11], 1), 0, GROUPS - 1).astype(jnp.int32),
        "coarsest": draw_coarsest(jax.random.fold_in(splits[13], 71), 0),
    }


omega = 0.7
highest = lax.Precision.HIGHEST


def weights_of(types, scales, kinds):
    chosen = (types[..., None] == jnp.arange(kinds, dtype=jnp.int32)).astype(jnp.float32)
    return chosen * scales[..., None], chosen


def lookup_rows(vector, weights, blocks):
    def one_row(operand):
        values, row_weights = operand
        products = jnp.einsum('yn,tmn->ytm', values, blocks, precision=highest)
        return jnp.sum(row_weights[..., None] * products, axis=1)
    return lax.map(one_row, (vector, weights))


def apply_grid(field, weights, blocks):
    padded = jnp.pad(field, ((1, 1), (1, 1), (0, 0)))
    summed = lookup_rows(field, weights[0], blocks[0])
    summed = summed + lookup_rows(padded[:-2, 1:-1], weights[1], blocks[1])
    summed = summed + lookup_rows(padded[2:, 1:-1], weights[2], blocks[2])
    summed = summed + lookup_rows(padded[1:-1, :-2], weights[3], blocks[3])
    return summed + lookup_rows(padded[1:-1, 2:], weights[4], blocks[4])


def smooth(residual_in, chosen, scales, blocks):
    return omega * (lookup_rows(residual_in, chosen, blocks) / scales[..., None])


def reference(rhs, active, fine_types, fine_scales, fine_table, fine_smoother, fine_groups, coarse_types, coarse_scales, coarse_table, coarse_smoother, coarse_groups, coarsest):
    inside = active.astype(jnp.float32)[..., None]
    fine_w, fine_pick = weights_of(fine_types, fine_scales, KINDS)
    coarse_w, coarse_pick = weights_of(coarse_types, coarse_scales, KINDS)
    rows_i = jnp.arange(NX, dtype=jnp.int32)[:, None]
    cols_j = jnp.arange(NY, dtype=jnp.int32)[None, :]
    coarse_i = (rows_i // TILE_X) * COARSE_X + fine_groups // COARSE_Y
    coarse_j = (cols_j // TILE_Y) * COARSE_Y + fine_groups % COARSE_Y
    fine_ids = (coarse_i * NYC + coarse_j).reshape(-1)
    level_i = jnp.arange(NXC, dtype=jnp.int32)[:, None]
    level_j = jnp.arange(NYC, dtype=jnp.int32)[None, :]
    level_ids = (((level_i // COARSE_X) * N_GY + level_j // COARSE_Y) * GROUPS + coarse_groups).reshape(-1)

    def fine_apply(field):
        return apply_grid(field, fine_w, fine_table)

    def coarse_apply(field):
        return apply_grid(field, coarse_w, coarse_table)

    def fine_smooth(residual_in):
        return inside * smooth(residual_in, fine_pick[0], fine_scales[0], fine_smoother)

    def coarse_smooth(residual_in):
        return smooth(residual_in, coarse_pick[0], coarse_scales[0], coarse_smoother)

    state = fine_smooth(rhs)
    for repeat in range(2):
        if repeat > 0:
            state = state + fine_smooth(rhs - fine_apply(state))
        level_rhs = inside * (rhs - fine_apply(state))
        first_rhs = jax.ops.segment_sum(level_rhs.reshape(-1, BLOCK), fine_ids, num_segments=NXC * NYC).reshape(NXC, NYC, BLOCK)
        first_fix = coarse_smooth(first_rhs)
        leftover = first_rhs - coarse_apply(first_fix)
        second_rhs = jax.ops.segment_sum(leftover.reshape(-1, BLOCK), level_ids, num_segments=N_GX * N_GY * GROUPS).reshape(N_GX, LEVEL_ROWS)
        second_fix = jnp.einsum('pkl,pl->pk', coarsest, second_rhs, precision=highest).reshape(-1, BLOCK)
        first_fix = first_fix + second_fix[level_ids].reshape(NXC, NYC, BLOCK)
        first_fix = first_fix + coarse_smooth(first_rhs - coarse_apply(first_fix))
        state = state + inside * first_fix.reshape(-1, BLOCK)[fine_ids].reshape(NX, NY, BLOCK)
        state = state + fine_smooth(rhs - fine_apply(state))
    final_residual = inside * (rhs - fine_apply(state))
    return state, final_residual
```

```python
import functools

import jax
import jax.numpy as jnp
from jax import lax
from jax.experimental import pallas as pl
from jax.experimental.pallas import tpu as pltpu
from jax.sharding import PartitionSpec as P

MESH = pl.DeviceIdType.MESH
F32 = jnp.float32
BF16 = jnp.bfloat16
OMEGA = 0.7

TOP = 3
ROWS = 14


def lanes_of(shape):
    return lax.broadcasted_iota(jnp.int32, shape, len(shape) - 1)


def roll(x, shift):
    shift = shift % x.shape[-1]
    return x if shift == 0 else pltpu.roll(x, shift, x.ndim - 1)


def halves(x):
    high = x.astype(BF16)
    low = (x - high.astype(F32)).astype(BF16)
    return jnp.concatenate([high, low], axis=0)


def dot(a, b):
    return jnp.dot(a, b, preferred_element_type=F32)


def pick(products, kind, scale):
    width = products.shape[1]
    y = products.reshape(4, 8, 8, width)
    kind = jnp.broadcast_to(kind[None], (8, 8, width))
    out = jnp.where(kind == 1.0, y[1], y[0])
    out = jnp.where(kind == 2.0, y[2], out)
    out = jnp.where(kind == 3.0, y[3], out)
    return (out * scale[None]).reshape(64, width)


def kernel(
    ngx, ngy,
    rhs_ref, active_ref, ftypes_ref, fscales_ref, ftab_ref, fsm_ref, fgroups_ref,
    ctypes_ref, cscales_ref, ctab_ref, csm_ref, cgroups_ref, coarsest_ref,
    sol_ref, res_ref,
    st, xa, xb, rhs_s, meta, gplane, tb, sb, c0b, fb, cplane, ctb, csb, cc0,
    ft, fs, ct, cs, member, lv, ff, m_s,
    e0_row, e0_col, e3_row, e3_col, e6_row, e6_col, ba_meta_row, ba_meta_col, ba_rhs_col, ba_rhs_row, ba_cg,
    e1_row, e1_col, rs_own, rs_up, rs_dn,
    pack_st, pack_rhs, pack_mrow, pack_mcol, cpack, parts, asm, onehot,
    load_sem, s0, r0, sb_sem, rb_sem, s1, r1, srs, rrs, rrsx, s3, r3, s6, r6, dis,
):
    gx = lax.axis_index("gx")
    gy = lax.axis_index("gy")
    up = (lax.rem(gx + ngx - 1, ngx), gy)
    down = (lax.rem(gx + 1, ngx), gy)
    left = (gx, lax.rem(gy + ngy - 1, ngy))
    right = (gx, lax.rem(gy + 1, ngy))
    has_up, has_down = gx > 0, gx < ngx - 1
    has_left, has_right = gy > 0, gy < ngy - 1

    barrier = pltpu.get_barrier_semaphore()
    for to in (up, down, left, right):
        pl.semaphore_signal(barrier, inc=1, device_id=to, device_id_type=MESH)

    load = pltpu.make_async_copy(coarsest_ref.at[0], m_s, load_sem)
    load.start()

    def send(src, dst, ssem, rsem, to):
        copy = pltpu.make_async_remote_copy(
            src_ref=src, dst_ref=dst, send_sem=ssem, recv_sem=rsem, device_id=to, device_id_type=MESH
        )
        copy.start()
        return copy

    def keep(flag, x):
        return jnp.where(flag, x, jnp.zeros_like(x))

    lane = lanes_of((64, 128))

    st[...] = jnp.zeros_like(st)
    xa[...] = jnp.zeros_like(xa)
    xb[...] = jnp.zeros_like(xb)
    rhs_s[...] = jnp.zeros_like(rhs_s)
    meta[...] = jnp.zeros_like(meta)
    gplane[...] = jnp.full_like(gplane, -1)
    cplane[...] = jnp.zeros_like(cplane)
    for i in range(8):
        rhs_s[TOP + i, :, 0:96] = rhs_ref[i]
    for d in range(5):
        meta[d, TOP:TOP + 8, 0:96] = ftypes_ref[d].astype(F32)
        meta[5 + d, TOP:TOP + 8, 0:96] = fscales_ref[d]
        cplane[d, 0:4, 0:48] = ctypes_ref[d].astype(F32)
        cplane[5 + d, 0:4, 0:48] = cscales_ref[d]
    meta[10, TOP:TOP + 8, 0:96] = active_ref[...].astype(F32)
    g = fgroups_ref[...]
    step = lambda k: (g >= 48 * k).astype(jnp.int32)
    gplane[0:8, 0:96] = g + 16 * (step(1) + step(2) + step(3))
    cplane[10, 0:4, 0:48] = (cgroups_ref[...] + 1).astype(F32)

    def split_table(block):
        high = block.astype(BF16).astype(F32)
        low = block - high
        return jnp.concatenate([high, high, low, low], axis=1).astype(BF16)

    fs[...] = split_table(fsm_ref[...].reshape(256, 64))
    cs[...] = split_table(csm_ref[...].reshape(256, 64))
    for d in range(5):
        ft[d] = split_table(ftab_ref[d].reshape(256, 64))
        ct[d] = split_table(ctab_ref[d].reshape(256, 64))

    def weights(rows):
        for a in rows:
            for d in range(5):
                shift = {3: -1, 4: 1}.get(d, 0)
                tb[d, a] = jnp.broadcast_to(roll(meta[d, a:a + 1, :], shift), (8, 128))
                sb[d, a] = jnp.broadcast_to(roll(meta[5 + d, a:a + 1, :], shift), (8, 128))
            scale = meta[5, a:a + 1, :]
            inside = meta[10, a:a + 1, :]
            factor = jnp.where(scale > 0.0, OMEGA * inside / jnp.where(scale > 0.0, scale, 1.0), 0.0)
            c0b[a] = jnp.broadcast_to(factor, (8, 128))
            fb[a] = jnp.broadcast_to(inside, (8, 128))

    weights(range(TOP, TOP + 8))

    def both(ref, a):
        return jnp.concatenate([ref[a], ref[a + 1]], axis=-1)

    def rhs_operand(x, a):
        pair = both(x, a)
        return jnp.concatenate([pair, pair], axis=0)

    def apply_pair(x, a):
        kinds = lambda d: jnp.concatenate([tb[d, a], tb[d, a + 1]], axis=-1)
        scales = lambda d: jnp.concatenate([sb[d, a], sb[d, a + 1]], axis=-1)
        here = rhs_operand(x, a)
        out = pick(dot(ft[0], here), kinds(0), scales(0))
        out = out + pick(dot(ft[1], rhs_operand(x, a - 1)), kinds(1), scales(1))
        out = out + pick(dot(ft[2], rhs_operand(x, a + 1)), kinds(2), scales(2))
        for d, shift in ((3, 1), (4, -1)):
            part = pick(dot(ft[d], here), kinds(d), scales(d))
            out = out + jnp.concatenate([roll(part[:, :128], shift), roll(part[:, 128:], shift)], axis=-1)
        return out

    def smooth_pair(r, a):
        parts2 = halves(r)
        y = dot(fs[...], jnp.concatenate([parts2, parts2], axis=0))
        kind = jnp.concatenate([tb[0, a], tb[0, a + 1]], axis=-1)
        factor = jnp.concatenate([c0b[a], c0b[a + 1]], axis=-1)
        return pick(y, kind, factor)

    def put(x, a, value):
        x[a] = halves(value)

    def smooth_rows(source, target, first, pairs):
        def body(k, carry):
            a = first + 2 * k
            r = both(rhs_s, a) - apply_pair(source, a)
            new = both(st, a) + smooth_pair(r, a)
            for n in range(2):
                part = new[:, 128 * n:128 * n + 128]
                st[a + n] = part
                put(target, a + n, part)
            return carry
        lax.fori_loop(0, pairs, body, 0)

    def level_rows(source):
        def body(k, carry):
            a = TOP + 2 * k
            inside = jnp.concatenate([fb[a], fb[a + 1]], axis=-1)
            r = (both(rhs_s, a) - apply_pair(source, a)).reshape(8, 8, 256) * inside[None]
            lv[k] = halves(r.reshape(64, 256))
            return carry
        lax.fori_loop(0, 4, body, 0)

    def first_body(k, carry):
        a = TOP + 2 * k
        new = smooth_pair(both(rhs_s, a), a)
        for n in range(2):
            part = new[:, 128 * n:128 * n + 128]
            st[a + n] = part
            put(xa, a + n, part)
        return carry

    lax.fori_loop(0, 4, first_body, 0)

    def pack_columns(field, slot, out):
        first = jnp.zeros((64, 128), F32)
        last = jnp.zeros((64, 128), F32)
        for i in range(8):
            block = field[TOP + i]
            mask = (lane >= 4 * i) & (lane < 4 * i + 3)
            first = jnp.where(mask, roll(block, 4 * i), first)
            last = jnp.where(mask, roll(block, 4 * i - 93), last)
        out[slot] = first
        out[slot + 1] = last

    def with_columns(block, from_left, from_right, i):
        block = jnp.where((lane >= 96) & (lane < 99), roll(from_right, 96 - 4 * i), block)
        return jnp.where(lane >= 125, roll(from_left, 125 - 4 * i), block)

    pack_columns(st, 0, pack_st)
    pl.semaphore_wait(barrier, 4)
    e0 = [
        send(st.at[TOP], e0_row.at[1], s0.at[0], r0.at[1], up),
        send(st.at[TOP + 7], e0_row.at[0], s0.at[1], r0.at[0], down),
        send(pack_st.at[0], e0_col.at[1], s0.at[2], r0.at[3], left),
        send(pack_st.at[1], e0_col.at[0], s0.at[3], r0.at[2], right),
    ]

    row256 = lax.broadcasted_iota(jnp.int32, (256, 128), 0)
    for i in range(8):
        code = jnp.broadcast_to(gplane[i:i + 1, :], (256, 128))
        member[:, 128 * i:128 * i + 128] = jnp.where(row256 == code, 1.0, 0.0).astype(BF16)

    cweights = []
    for k in range(11):
        plane = cplane[k]
        low = plane[0:1, :] + roll(plane[1:2, :], 64)
        high = plane[2:3, :] + roll(plane[3:4, :], 64)
        cweights.append((low, high))
    for d in range(5):
        shift = {3: -1, 4: 1}.get(d, 0)
        for n in range(2):
            ctb[d, :, 128 * n:128 * n + 128] = jnp.broadcast_to(roll(cweights[d][n], shift), (8, 128))
            csb[d, :, 128 * n:128 * n + 128] = jnp.broadcast_to(roll(cweights[5 + d][n], shift), (8, 128))
    for n in range(2):
        scale = cweights[5][n]
        factor = jnp.where(scale > 0.0, OMEGA / jnp.where(scale > 0.0, scale, 1.0), 0.0)
        cc0[:, 128 * n:128 * n + 128] = jnp.broadcast_to(factor, (8, 128))
    cpack[...] = jnp.concatenate([cweights[10][0], cweights[10][1], jnp.zeros((6, 128), F32)], axis=0)

    for k in range(11):
        pack_mrow[0, 2 * k:2 * k + 2, :] = meta[k, TOP:TOP + 2, :]
        pack_mrow[1, 2 * k:2 * k + 2, :] = meta[k, TOP + 6:TOP + 8, :]
    pack_mrow[0, 22:24, :] = jnp.zeros((2, 128), F32)
    pack_mrow[1, 22:24, :] = jnp.zeros((2, 128), F32)
    lane8 = lanes_of((8, 128))
    first = jnp.zeros((8, 128), F32)
    last = jnp.zeros((8, 128), F32)
    for k in range(11):
        block = meta[k, TOP:TOP + 8, :]
        mask = (lane8 >= 2 * k) & (lane8 < 2 * k + 2)
        first = jnp.where(mask, roll(block, 2 * k), first)
        last = jnp.where(mask, roll(block, 2 * k - 94), last)
    pack_mcol[0] = first
    pack_mcol[1] = last
    pack_columns(rhs_s, 0, pack_rhs)

    for copy in e0:
        copy.wait_recv()
    put(xa, TOP - 1, keep(has_up, e0_row[0]))
    put(xa, TOP + 8, keep(has_down, e0_row[1]))
    from_left = keep(has_left, e0_col[0])
    from_right = keep(has_right, e0_col[1])
    for i in range(8):
        put(xa, TOP + i, with_columns(st[TOP + i], from_left, from_right, i))
    for k, hop in enumerate((2, -2)):
        pl.semaphore_signal(dis.at[0], inc=1, device_id=(gx, lax.rem(gy + ngy + hop, ngy)), device_id_type=MESH)

    low_half = lane < 64

    def coarse_operands(c0, c1, top, bottom):
        swapped0, swapped1 = roll(c0, 64), roll(c1, 64)
        middle = jnp.where(low_half, swapped0, swapped1)
        before0 = jnp.where(low_half, top, swapped0)
        after1 = jnp.where(low_half, swapped1, bottom)
        def operand(p, q):
            h = halves(jnp.concatenate([p, q], axis=1))
            return jnp.concatenate([h, h], axis=0)
        return operand(c0, c1), operand(before0, middle), operand(middle, after1)

    def coarse_apply(c0, c1, top, bottom):
        here, before, after = coarse_operands(c0, c1, top, bottom)
        out = pick(dot(ct[0], here), ctb[0], csb[0])
        out = out + pick(dot(ct[1], before), ctb[1], csb[1])
        out = out + pick(dot(ct[2], after), ctb[2], csb[2])
        for d, shift in ((3, 1), (4, -1)):
            part = pick(dot(ct[d], here), ctb[d], csb[d])
            out = out + jnp.concatenate([roll(part[:, :128], shift), roll(part[:, 128:], shift)], axis=-1)
        return out

    def coarse_smooth(r):
        h = halves(r)
        return pick(dot(cs[...], jnp.concatenate([h, h], axis=0)), ctb[0], cc0)

    left_lanes = (lane == 127) | (lane == 63)
    right_lanes = (lane == 48) | (lane == 112)

    def background():
        copies = [
            send(rhs_s.at[pl.ds(TOP, 2)], ba_rhs_row.at[1], sb_sem.at[0], rb_sem.at[0], up),
            send(rhs_s.at[pl.ds(TOP + 6, 2)], ba_rhs_row.at[0], sb_sem.at[1], rb_sem.at[1], down),
            send(pack_mrow.at[0], ba_meta_row.at[1], sb_sem.at[2], rb_sem.at[2], up),
            send(pack_mrow.at[1], ba_meta_row.at[0], sb_sem.at[3], rb_sem.at[3], down),
        ]
        slot = 4
        for k, x in enumerate((gx, up[0], down[0])):
            for side, to in ((0, left[1]), (1, right[1])):
                copies.append(send(pack_mcol.at[side], ba_meta_col.at[k, side], sb_sem.at[slot], rb_sem.at[slot], (x, to)))
                copies.append(
                    send(pack_rhs.at[side], ba_rhs_col.at[k, side], sb_sem.at[slot + 1], rb_sem.at[slot + 1], (x, to))
                )
                slot += 2
        for k, to in enumerate((down, up, right, left)):
            copies.append(send(cpack, ba_cg.at[k], sb_sem.at[slot + k], rb_sem.at[slot + k], to))
        return copies

    def disseminate(level, hop):
        pl.semaphore_wait(dis.at[level], 2)
        if hop:
            for h in (hop, -hop):
                pl.semaphore_signal(
                    dis.at[level + 1], inc=1, device_id=(gx, lax.rem(gy + ngy + h, ngy)), device_id_type=MESH
                )

    def unpack_groups():
        lane1 = lanes_of((1, 128))
        is_left = (lane1 == 127) | (lane1 == 63)
        is_right = (lane1 == 48) | (lane1 == 112)
        codes = []
        for n in range(2):
            own = cpack[n:n + 1, :]
            code = jnp.where(own > 0.0, 8.0 * (own - 1.0), -1.0)
            fl = roll(ba_cg[2, n:n + 1, :], 80)
            fr = roll(ba_cg[3, n:n + 1, :], 48)
            code = jnp.where(is_left & has_left, 8.0 * (fl - 1.0) + 1.0, code)
            code = jnp.where(is_right & has_right, 8.0 * (fr - 1.0) + 2.0, code)
            codes.append(code)
        top = roll(ba_cg[0, 1:2, :], 64)
        bottom = roll(ba_cg[1, 0:1, :], 64)
        ends = jnp.full((1, 128), -1.0, F32)
        ends = jnp.where((lane1 < 48) & has_up, 8.0 * (top - 1.0) + 3.0, ends)
        ends = jnp.where((lane1 >= 64) & (lane1 < 112) & has_down, 8.0 * (bottom - 1.0) + 4.0, ends)
        codes.append(ends)
        rows = lax.broadcasted_iota(jnp.int32, (128, 128), 0)
        entry = jnp.where(rows < 32, lax.rem(rows, 16), 99).astype(F32)
        for n in range(3):
            hit = entry == jnp.broadcast_to(codes[n], (128, 128))
            onehot[:, 128 * n:128 * n + 128] = jnp.where(hit, 1.0, 0.0).astype(BF16)

    def unpack_halo():
        lane16 = lanes_of((16, 128))
        flags = ((has_left, has_right), (has_up, has_down))
        asm[...] = jnp.zeros_like(asm)
        for side in range(2):
            asm[side, 3:11, :] = ba_meta_col[0, side]
            asm[side, 1:3, :] = ba_meta_col[2, side, 6:8, :]
            asm[side, 11:13, :] = ba_meta_col[1, side, 0:2, :]
        for k in range(11):
            for rows, side, flag in ((slice(1, 3), 0, has_up), (slice(11, 13), 1, has_down)):
                block = ba_meta_row[side, 2 * k:2 * k + 2, :]
                meta[k, rows, :] = keep(flag, block) if k == 10 else block
            block = meta[k]
            fr = roll(asm[0], 96 - 2 * k)
            fl = roll(asm[1], 126 - 2 * k)
            if k == 10:
                fr, fl = keep(has_right, fr), keep(has_left, fl)
                row = lax.broadcasted_iota(jnp.int32, (16, 128), 0)
                dead = ((row < 3) & jnp.logical_not(has_up)) | ((row > 10) & jnp.logical_not(has_down))
                fr, fl = jnp.where(dead, 0.0, fr), jnp.where(dead, 0.0, fl)
            block = jnp.where((lane16 >= 96) & (lane16 < 98), fr, block)
            meta[k] = jnp.where(lane16 >= 126, fl, block)
        for a in range(1, 13):
            if a < 3:
                block, source, i = ba_rhs_row[0, a - 1], 2, a + 5
            elif a < 11:
                block, source, i = rhs_s[a], 0, a - 3
            else:
                block, source, i = ba_rhs_row[1, a - 11], 1, a - 11
            rhs_s[a] = with_columns(block, ba_rhs_col[source, 1], ba_rhs_col[source, 0], i)
        weights(range(1, 13))

    behind = []
    e1_sent = []

    def taken(count, rows, sem):
        shape = rs_own.at[0, pl.ds(0, count), pl.ds(0, rows)]
        pltpu.make_async_copy(shape, shape, sem).wait()

    def correct(cycle):
        summed = jnp.zeros((128, 256), F32)
        for k in range(4):
            summed = summed + lax.dot_general(
                lv[k], member[:, 256 * k:256 * k + 256], (((1,), (1,)), ((), ())), preferred_element_type=F32
            )
        first_rhs = summed[:64] + summed[64:]
        fix = coarse_smooth(first_rhs)
        f0, f1 = fix[:, :128], fix[:, 128:]
        ff[cycle, 0] = f0
        ff[cycle, 1] = f1
        ff[cycle, 2] = jnp.where(
            (lane == 0) | (lane == 64), f0, jnp.where((lane == 1) | (lane == 65), roll(f1, 1), 0.0)
        )
        ff[cycle, 3] = jnp.where(
            (lane == 47) | (lane == 111), f0, jnp.where((lane == 48) | (lane == 112), roll(f1, 1), 0.0)
        )
        e1 = [
            send(ff.at[cycle, 0], e1_row.at[cycle, 1], s1.at[cycle, 0], r1.at[cycle, 1], up),
            send(ff.at[cycle, 1], e1_row.at[cycle, 0], s1.at[cycle, 1], r1.at[cycle, 0], down),
            send(ff.at[cycle, 2], e1_col.at[cycle, 1], s1.at[cycle, 2], r1.at[cycle, 3], left),
            send(ff.at[cycle, 3], e1_col.at[cycle, 0], s1.at[cycle, 3], r1.at[cycle, 2], right),
        ]
        e1_sent.extend(e1)
        if cycle == 0:
            behind.extend(background())
            disseminate(0, 4)
            disseminate(1, 1)
        for copy in e1:
            copy.wait_recv()
        top = roll(keep(has_up, e1_row[cycle, 0]), 64)
        bottom = roll(keep(has_down, e1_row[cycle, 1]), 64)
        fl = keep(has_left, e1_col[cycle, 0])
        fr = keep(has_right, e1_col[cycle, 1])
        h0 = jnp.where(left_lanes, roll(fl, 80), jnp.where(right_lanes, roll(fr, 48), f0))
        h1 = jnp.where(left_lanes, roll(fl, 79), jnp.where(right_lanes, roll(fr, 47), f1))
        leftover = first_rhs - coarse_apply(h0, h1, top, bottom)
        l0, l1 = leftover[:, :128], leftover[:, 128:]
        entries = []
        for h in range(2):
            m0 = jnp.broadcast_to(cpack[0:1, :] == h + 1.0, (64, 128))
            m1 = jnp.broadcast_to(cpack[1:2, :] == h + 1.0, (64, 128))
            total = jnp.where(m0, l0, 0.0) + jnp.where(m1, l1, 0.0)
            entries.append(jnp.sum(total, axis=1, keepdims=True))
        column = jnp.broadcast_to(jnp.concatenate(entries, axis=0), (128, 128))
        if cycle == 0:
            load.wait()
        for q in range(ngy):
            row = jnp.sum(m_s[:, 128 * q:128 * q + 128] * column, axis=0, keepdims=True)
            parts[cycle, q, 0:1, :] = row
            if q + 1 < ngy:
                parts[cycle, q + 1, 1:2, :] = row
            if q > 0:
                parts[cycle, q - 1, 2:3, :] = row
        parts[cycle, 0, 1:2, :] = jnp.zeros((1, 128), F32)
        parts[cycle, ngy - 1, 2:3, :] = jnp.zeros((1, 128), F32)
        if cycle == 0:
            disseminate(2, 0)

        def own_copy(k):
            q = lax.rem(gy + k, ngy)
            return pltpu.make_async_remote_copy(
                src_ref=parts.at[cycle, q, pl.ds(0, 3)], dst_ref=rs_own.at[cycle, gy, pl.ds(0, 3)],
                send_sem=srs.at[cycle, 0], recv_sem=rrs.at[cycle], device_id=(gx, q), device_id_type=MESH,
            )

        def cross_copy(k, which):
            q = lax.rem(gy + k, ngy)
            to, dst = (up[0], rs_dn) if which == 0 else (down[0], rs_up)
            return pltpu.make_async_remote_copy(
                src_ref=parts.at[cycle, q, pl.ds(0, 1)], dst_ref=dst.at[cycle, gy, pl.ds(0, 1)],
                send_sem=srs.at[cycle, 1 + which], recv_sem=rrsx.at[cycle, which], device_id=(to, q), device_id_type=MESH,
            )

        for k in range(1, ngy):
            own_copy(k).start()
        for k in range(ngy):
            cross_copy(k, 0).start()
            cross_copy(k, 1).start()
        rs_own[cycle, gy, 0:3, :] = parts[cycle, gy, 0:3, :]
        if cycle == 0:
            for copy in behind:
                copy.wait()
            unpack_groups()
            unpack_halo()
        taken(ngy - 1, 3, rrs.at[cycle])
        taken(ngy, 1, rrsx.at[cycle, 0])
        taken(ngy, 1, rrsx.at[cycle, 1])
        own = rs_own[cycle, 0, 0:3, :]
        above = rs_up[cycle, 0, 0:1, :]
        below = rs_dn[cycle, 0, 0:1, :]
        for q in range(1, ngy):
            own = own + rs_own[cycle, q, 0:3, :]
            above = above + rs_up[cycle, q, 0:1, :]
            below = below + rs_dn[cycle, q, 0:1, :]
        five = jnp.concatenate([own, above, below, jnp.zeros((3, 128), F32)], axis=0)
        both_groups = jnp.concatenate([five, roll(five, 64)], axis=0)
        high = both_groups.astype(BF16).astype(F32)
        tall = jnp.concatenate([high, both_groups - high, jnp.zeros((96, 128), F32)], axis=0)
        lifted = dot(tall.T[0:64].astype(BF16), onehot[...])
        p0, p1, ends = lifted[:, :128], lifted[:, 128:256], lifted[:, 256:]
        rest = leftover - coarse_apply(p0, p1, ends, ends)
        fix = fix + lifted[:, :256] + coarse_smooth(rest)
        spread = dot(halves(fix), member[...])
        spread = spread[:64] + spread[64:]
        for i in range(8):
            block = spread[:, 128 * i:128 * i + 128].reshape(8, 8, 128) * fb[TOP + i][None]
            st[TOP + i] = st[TOP + i] + block.reshape(64, 128)

    def exchange(width, row_buf, col_buf, ssem, rsem, slot):
        pack_columns(st, slot, pack_st)
        copies = [
            send(st.at[pl.ds(TOP, width)], row_buf.at[1], ssem.at[0], rsem.at[1], up),
            send(st.at[pl.ds(TOP + 8 - width, width)], row_buf.at[0], ssem.at[1], rsem.at[0], down),
        ]
        n = 2
        for k, x in enumerate((gx, up[0], down[0])):
            for side, to in ((0, left[1]), (1, right[1])):
                copies.append(send(pack_st.at[slot + side], col_buf.at[k, side], ssem.at[n], rsem.at[n], (x, to)))
                n += 1
        for copy in copies:
            copy.wait()
        for a in range(TOP - width, TOP + 8 + width):
            if a < 3:
                block, source, i, flag = row_buf[0, a - (TOP - width)], 2, a + 5, has_up
            elif a < 11:
                block, source, i, flag = st[a], 0, a - 3, None
            else:
                block, source, i, flag = row_buf[1, a - 11], 1, a - 11, has_down
            fl = keep(has_left, col_buf[source, 1])
            fr = keep(has_right, col_buf[source, 0])
            block = with_columns(block, fl, fr, i)
            if flag is not None:
                block = keep(flag, block)
            st[a] = block
            put(xa, a, block)

    level_rows(xa)
    for copy in e0:
        copy.wait_send()
    correct(0)
    exchange(3, e3_row, e3_col, s3, r3, 2)
    smooth_rows(xa, xb, 1, 6)
    smooth_rows(xb, xa, 2, 5)
    level_rows(xa)
    correct(1)
    exchange(2, e6_row, e6_col, s6, r6, 4)
    smooth_rows(xa, xb, 2, 5)

    def final_body(k, carry):
        a = TOP + 2 * k
        inside = jnp.concatenate([fb[a], fb[a + 1]], axis=-1)
        r = (both(rhs_s, a) - apply_pair(xb, a)).reshape(8, 8, 256) * inside[None]
        r = r.reshape(64, 256)
        for n in range(2):
            res_ref[2 * k + n] = r[:, 128 * n:128 * n + 96]
            sol_ref[2 * k + n] = st[a + n][:, 0:96]
        return carry

    lax.fori_loop(0, 4, final_body, 0)

    for copy in e1_sent:
        copy.wait_send()
    for cycle in range(2):
        taken(ngy - 1, 3, srs.at[cycle, 0])
        taken(ngy, 1, srs.at[cycle, 1])
        taken(ngy, 1, srs.at[cycle, 2])


def solution(mesh):
    ngx, ngy = mesh.shape["gx"], mesh.shape["gy"]

    def shards(
        rhs, active, fine_types, fine_scales, fine_table, fine_smoother, fine_groups,
        coarse_types, coarse_scales, coarse_table, coarse_smoother, coarse_groups, coarsest,
    ):
        vmem = pl.BlockSpec(memory_space=pltpu.VMEM)
        field = jax.ShapeDtypeStruct((8, 64, 96), F32)
        dma = pltpu.SemaphoreType.DMA
        sol, res = pl.pallas_call(
            functools.partial(kernel, ngx, ngy),
            out_shape=(field, field),
            in_specs=[vmem] * 12 + [pl.BlockSpec(memory_space=pl.ANY)],
            out_specs=(vmem, vmem),
            scratch_shapes=[
                pltpu.VMEM((ROWS, 64, 128), F32),
                pltpu.VMEM((ROWS, 128, 128), BF16),
                pltpu.VMEM((ROWS, 128, 128), BF16),
                pltpu.VMEM((ROWS, 64, 128), F32),
                pltpu.VMEM((11, 16, 128), F32),
                pltpu.VMEM((8, 128), jnp.int32),
                pltpu.VMEM((5, ROWS, 8, 128), F32),
                pltpu.VMEM((5, ROWS, 8, 128), F32),
                pltpu.VMEM((ROWS, 8, 128), F32),
                pltpu.VMEM((ROWS, 8, 128), F32),
                pltpu.VMEM((11, 8, 128), F32),
                pltpu.VMEM((5, 8, 256), F32),
                pltpu.VMEM((5, 8, 256), F32),
                pltpu.VMEM((8, 256), F32),
                pltpu.VMEM((5, 256, 256), BF16),
                pltpu.VMEM((256, 256), BF16),
                pltpu.VMEM((5, 256, 256), BF16),
                pltpu.VMEM((256, 256), BF16),
                pltpu.VMEM((256, 1024), BF16),
                pltpu.VMEM((4, 128, 256), BF16),
                pltpu.VMEM((2, 4, 64, 128), F32),
                pltpu.VMEM((128, 128 * ngy), F32),
                pltpu.VMEM((2, 64, 128), F32),
                pltpu.VMEM((2, 64, 128), F32),
                pltpu.VMEM((2, 3, 64, 128), F32),
                pltpu.VMEM((3, 2, 64, 128), F32),
                pltpu.VMEM((2, 2, 64, 128), F32),
                pltpu.VMEM((3, 2, 64, 128), F32),
                pltpu.VMEM((2, 24, 128), F32),
                pltpu.VMEM((3, 2, 8, 128), F32),
                pltpu.VMEM((3, 2, 64, 128), F32),
                pltpu.VMEM((2, 2, 64, 128), F32),
                pltpu.VMEM((4, 8, 128), F32),
                pltpu.VMEM((2, 2, 64, 128), F32),
                pltpu.VMEM((2, 2, 64, 128), F32),
                pltpu.VMEM((2, ngy, 8, 128), F32),
                pltpu.VMEM((2, ngy, 8, 128), F32),
                pltpu.VMEM((2, ngy, 8, 128), F32),
                pltpu.VMEM((6, 64, 128), F32),
                pltpu.VMEM((2, 64, 128), F32),
                pltpu.VMEM((2, 24, 128), F32),
                pltpu.VMEM((2, 8, 128), F32),
                pltpu.VMEM((8, 128), F32),
                pltpu.VMEM((2, ngy, 8, 128), F32),
                pltpu.VMEM((2, 16, 128), F32),
                pltpu.VMEM((128, 384), BF16),
                dma,
                dma((4,)), dma((4,)),
                dma((20,)), dma((20,)),
                dma((2, 4)), dma((2, 4)),
                dma((2, 3)), dma((2,)), dma((2, 2)),
                dma((8,)), dma((8,)),
                dma((8,)), dma((8,)),
                pltpu.SemaphoreType.REGULAR((3,)),
            ],
            compiler_params=pltpu.CompilerParams(
                collective_id=0, has_side_effects=True, vmem_limit_bytes=48 * 2**20
            ),
        )(
            jnp.swapaxes(rhs, 1, 2), active, fine_types, fine_scales, fine_table, fine_smoother, fine_groups,
            coarse_types, coarse_scales, coarse_table, coarse_smoother, coarse_groups, coarsest,
        )
        return jnp.swapaxes(sol, 1, 2), jnp.swapaxes(res, 1, 2)

    return jax.shard_map(
        shards,
        mesh=mesh,
        in_specs=(
            P("gx", "gy", None),
            P("gx", "gy"),
            P(None, "gx", "gy"),
            P(None, "gx", "gy"),
            P(),
            P(),
            P("gx", "gy"),
            P(None, "gx", "gy"),
            P(None, "gx", "gy"),
            P(),
            P(),
            P("gx", "gy"),
            P("gx", "gy", None),
        ),
        out_specs=(P("gx", "gy", None), P("gx", "gy", None)),
        check_vma=False,
    )
```

```python
import functools

import jax
import jax.numpy as jnp
from jax import lax
from jax.experimental import pallas as pl
from jax.experimental.pallas import tpu as pltpu
from jax.sharding import PartitionSpec as P

MESH = pl.DeviceIdType.MESH
F32 = jnp.float32
BF16 = jnp.bfloat16
OMEGA = 0.7

TOP = 3
ROWS = 14


def lanes_of(shape):
    return lax.broadcasted_iota(jnp.int32, shape, len(shape) - 1)


def roll(x, shift):
    shift = shift % x.shape[-1]
    return x if shift == 0 else pltpu.roll(x, shift, x.ndim - 1)


def halves(x):
    high = x.astype(BF16)
    low = (x - high.astype(F32)).astype(BF16)
    return jnp.concatenate([high, low], axis=0)


def dot(a, b):
    return jnp.dot(a, b, preferred_element_type=F32)


def pick(products, kind, scale):
    width = products.shape[1]
    y = products.reshape(4, 8, 8, width)
    kind = jnp.broadcast_to(kind[None], (8, 8, width))
    out = jnp.where(kind == 1.0, y[1], y[0])
    out = jnp.where(kind == 2.0, y[2], out)
    out = jnp.where(kind == 3.0, y[3], out)
    return (out * scale[None]).reshape(64, width)


def kernel(
    ngx, ngy,
    rhs_in, active_in, ftypes_in, fscales_in, ftab_in, fsm_in, fgroups_in,
    ctypes_in, cscales_in, ctab_in, csm_in, cgroups_in, coarsest_in,
    sol_ref, res_ref,
    rhs_ref, active_ref, ftypes_ref, fscales_ref, ftab_ref, fsm_ref, fgroups_ref,
    ctypes_ref, cscales_ref, ctab_ref, csm_ref, cgroups_ref,
    st, xa, xb, rhs_s, meta, gplane, tb, sb, c0b, fb, cplane, ctb, csb, cc0,
    ft, fs, ct, cs, member, lv, ff, m_s,
    e0_row, e0_col, e3_row, e3_col, e6_row, e6_col, ba_meta_row, ba_meta_col, ba_rhs_col, ba_rhs_row, ba_cg,
    e1_row, e1_col, rs_own, rs_up, rs_dn,
    pack_st, pack_rhs, pack_mrow, pack_mcol, cpack, parts, asm, onehot,
    load_sem, s0, r0, sb_sem, rb_sem, s1, r1, srs, rrs, rrsx, s3, r3, s6, r6, dis,
):
    gx = lax.axis_index("gx")
    gy = lax.axis_index("gy")
    up = (lax.rem(gx + ngx - 1, ngx), gy)
    down = (lax.rem(gx + 1, ngx), gy)
    left = (gx, lax.rem(gy + ngy - 1, ngy))
    right = (gx, lax.rem(gy + 1, ngy))
    has_up, has_down = gx > 0, gx < ngx - 1
    has_left, has_right = gy > 0, gy < ngy - 1

    barrier = pltpu.get_barrier_semaphore()
    for to in (up, down, left, right):
        pl.semaphore_signal(barrier, inc=1, device_id=to, device_id_type=MESH)

    loads = [
        pltpu.make_async_copy(source, target, load_sem.at[n])
        for n, (source, target) in enumerate((
            (rhs_in, rhs_ref), (active_in, active_ref), (ftypes_in, ftypes_ref), (fscales_in, fscales_ref),
            (fsm_in, fsm_ref), (ftab_in, ftab_ref), (fgroups_in, fgroups_ref), (ctypes_in, ctypes_ref),
            (cscales_in, cscales_ref), (ctab_in, ctab_ref), (csm_in, csm_ref), (cgroups_in, cgroups_ref),
            (coarsest_in.at[0], m_s),
        ))
    ]
    for copy in loads:
        copy.start()

    def send(src, dst, ssem, rsem, to):
        copy = pltpu.make_async_remote_copy(
            src_ref=src, dst_ref=dst, send_sem=ssem, recv_sem=rsem, device_id=to, device_id_type=MESH
        )
        copy.start()
        return copy

    def keep(flag, x):
        return jnp.where(flag, x, jnp.zeros_like(x))

    lane = lanes_of((64, 128))

    st[...] = jnp.zeros_like(st)
    xa[...] = jnp.zeros_like(xa)
    xb[...] = jnp.zeros_like(xb)
    rhs_s[...] = jnp.zeros_like(rhs_s)
    meta[...] = jnp.zeros_like(meta)
    for copy in loads[:5]:
        copy.wait()
    for i in range(8):
        rhs_s[TOP + i, :, 0:96] = rhs_ref[i]
    for d in range(5):
        meta[d, TOP:TOP + 8, 0:96] = ftypes_ref[d].astype(F32)
        meta[5 + d, TOP:TOP + 8, 0:96] = fscales_ref[d]
    meta[10, TOP:TOP + 8, 0:96] = active_ref[...].astype(F32)
    def split_table(block):
        high = block.astype(BF16).astype(F32)
        low = block - high
        return jnp.concatenate([high, high, low, low], axis=1).astype(BF16)

    fs[...] = split_table(fsm_ref[...].reshape(256, 64))

    def weights(rows):
        for a in rows:
            for d in range(5):
                shift = {3: -1, 4: 1}.get(d, 0)
                tb[d, a] = jnp.broadcast_to(roll(meta[d, a:a + 1, :], shift), (8, 128))
                sb[d, a] = jnp.broadcast_to(roll(meta[5 + d, a:a + 1, :], shift), (8, 128))
            scale = meta[5, a:a + 1, :]
            inside = meta[10, a:a + 1, :]
            factor = jnp.where(scale > 0.0, OMEGA * inside / jnp.where(scale > 0.0, scale, 1.0), 0.0)
            c0b[a] = jnp.broadcast_to(factor, (8, 128))
            fb[a] = jnp.broadcast_to(inside, (8, 128))

    weights(range(TOP, TOP + 8))

    def both(ref, a):
        return jnp.concatenate([ref[a], ref[a + 1]], axis=-1)

    def rhs_operand(x, a):
        pair = both(x, a)
        return jnp.concatenate([pair, pair], axis=0)

    def apply_pair(x, a):
        kinds = lambda d: jnp.concatenate([tb[d, a], tb[d, a + 1]], axis=-1)
        scales = lambda d: jnp.concatenate([sb[d, a], sb[d, a + 1]], axis=-1)
        here = rhs_operand(x, a)
        out = pick(dot(ft[0], here), kinds(0), scales(0))
        out = out + pick(dot(ft[1], rhs_operand(x, a - 1)), kinds(1), scales(1))
        out = out + pick(dot(ft[2], rhs_operand(x, a + 1)), kinds(2), scales(2))
        for d, shift in ((3, 1), (4, -1)):
            part = pick(dot(ft[d], here), kinds(d), scales(d))
            out = out + jnp.concatenate([roll(part[:, :128], shift), roll(part[:, 128:], shift)], axis=-1)
        return out

    def smooth_pair(r, a):
        parts2 = halves(r)
        y = dot(fs[...], jnp.concatenate([parts2, parts2], axis=0))
        kind = jnp.concatenate([tb[0, a], tb[0, a + 1]], axis=-1)
        factor = jnp.concatenate([c0b[a], c0b[a + 1]], axis=-1)
        return pick(y, kind, factor)

    def put(x, a, value):
        x[a] = halves(value)

    def smooth_rows(source, target, first, pairs):
        def body(k, carry):
            a = first + 2 * k
            r = both(rhs_s, a) - apply_pair(source, a)
            new = both(st, a) + smooth_pair(r, a)
            for n in range(2):
                part = new[:, 128 * n:128 * n + 128]
                st[a + n] = part
                put(target, a + n, part)
            return carry
        lax.fori_loop(0, pairs, body, 0, unroll=True)

    def level_rows(source):
        def body(k, carry):
            a = TOP + 2 * k
            inside = jnp.concatenate([fb[a], fb[a + 1]], axis=-1)
            r = (both(rhs_s, a) - apply_pair(source, a)).reshape(8, 8, 256) * inside[None]
            lv[k] = halves(r.reshape(64, 256))
            return carry
        lax.fori_loop(0, 4, body, 0, unroll=True)

    def first_body(k, carry):
        a = TOP + 2 * k
        new = smooth_pair(both(rhs_s, a), a)
        for n in range(2):
            part = new[:, 128 * n:128 * n + 128]
            st[a + n] = part
            put(xa, a + n, part)
        return carry

    lax.fori_loop(0, 4, first_body, 0, unroll=True)

    def pack_columns(field, slot, out):
        first = jnp.zeros((64, 128), F32)
        last = jnp.zeros((64, 128), F32)
        for i in range(8):
            block = field[TOP + i]
            mask = (lane >= 4 * i) & (lane < 4 * i + 3)
            first = jnp.where(mask, roll(block, 4 * i), first)
            last = jnp.where(mask, roll(block, 4 * i - 93), last)
        for n, block in ((0, first), (1, last)):
            out[slot + n] = sum(roll(block[16 * m:16 * m + 16], 32 * m) for m in range(4))

    def unfold(block):
        return jnp.concatenate([roll(block, -32 * m) for m in range(4)], axis=0)

    def with_columns(block, from_left, from_right, i):
        block = jnp.where((lane >= 96) & (lane < 99), roll(from_right, 96 - 4 * i), block)
        return jnp.where(lane >= 125, roll(from_left, 125 - 4 * i), block)

    pack_columns(st, 0, pack_st)
    pl.semaphore_wait(barrier, 4)
    e0 = [
        send(st.at[TOP], e0_row.at[1], s0.at[0], r0.at[1], up),
        send(st.at[TOP + 7], e0_row.at[0], s0.at[1], r0.at[0], down),
        send(pack_st.at[0], e0_col.at[1], s0.at[2], r0.at[3], left),
        send(pack_st.at[1], e0_col.at[0], s0.at[3], r0.at[2], right),
    ]

    for copy in loads[5:12]:
        copy.wait()
    cplane[...] = jnp.zeros_like(cplane)
    gplane[...] = jnp.full_like(gplane, -1)
    for d in range(5):
        cplane[d, 0:4, 0:48] = ctypes_ref[d].astype(F32)
        cplane[5 + d, 0:4, 0:48] = cscales_ref[d]
        ft[d] = split_table(ftab_ref[d].reshape(256, 64))
        ct[d] = split_table(ctab_ref[d].reshape(256, 64))
    cs[...] = split_table(csm_ref[...].reshape(256, 64))
    g = fgroups_ref[...]
    step = lambda k: (g >= 48 * k).astype(jnp.int32)
    gplane[0:8, 0:96] = g + 16 * (step(1) + step(2) + step(3))
    cplane[10, 0:4, 0:48] = (cgroups_ref[...] + 1).astype(F32)
    row256 = lax.broadcasted_iota(jnp.int32, (256, 128), 0)
    for i in range(8):
        code = jnp.broadcast_to(gplane[i:i + 1, :], (256, 128))
        member[:, 128 * i:128 * i + 128] = jnp.where(row256 == code, 1.0, 0.0).astype(BF16)

    cweights = []
    for k in range(11):
        plane = cplane[k]
        low = plane[0:1, :] + roll(plane[1:2, :], 64)
        high = plane[2:3, :] + roll(plane[3:4, :], 64)
        cweights.append((low, high))
    for d in range(5):
        shift = {3: -1, 4: 1}.get(d, 0)
        for n in range(2):
            ctb[d, :, 128 * n:128 * n + 128] = jnp.broadcast_to(roll(cweights[d][n], shift), (8, 128))
            csb[d, :, 128 * n:128 * n + 128] = jnp.broadcast_to(roll(cweights[5 + d][n], shift), (8, 128))
    for n in range(2):
        scale = cweights[5][n]
        factor = jnp.where(scale > 0.0, OMEGA / jnp.where(scale > 0.0, scale, 1.0), 0.0)
        cc0[:, 128 * n:128 * n + 128] = jnp.broadcast_to(factor, (8, 128))
    cpack[...] = jnp.concatenate([cweights[10][0], cweights[10][1], jnp.zeros((6, 128), F32)], axis=0)

    for k in range(11):
        pack_mrow[0, 2 * k:2 * k + 2, :] = meta[k, TOP:TOP + 2, :]
        pack_mrow[1, 2 * k:2 * k + 2, :] = meta[k, TOP + 6:TOP + 8, :]
    pack_mrow[0, 22:24, :] = jnp.zeros((2, 128), F32)
    pack_mrow[1, 22:24, :] = jnp.zeros((2, 128), F32)
    lane8 = lanes_of((8, 128))
    first = jnp.zeros((8, 128), F32)
    last = jnp.zeros((8, 128), F32)
    for k in range(11):
        block = meta[k, TOP:TOP + 8, :]
        mask = (lane8 >= 2 * k) & (lane8 < 2 * k + 2)
        first = jnp.where(mask, roll(block, 2 * k), first)
        last = jnp.where(mask, roll(block, 2 * k - 94), last)
    pack_mcol[0] = first
    pack_mcol[1] = last
    pack_columns(rhs_s, 0, pack_rhs)

    for copy in e0:
        copy.wait_recv()
    put(xa, TOP - 1, keep(has_up, e0_row[0]))
    put(xa, TOP + 8, keep(has_down, e0_row[1]))
    from_left = unfold(keep(has_left, e0_col[0]))
    from_right = unfold(keep(has_right, e0_col[1]))
    for i in range(8):
        put(xa, TOP + i, with_columns(st[TOP + i], from_left, from_right, i))
    for k, hop in enumerate((2, -2)):
        pl.semaphore_signal(dis.at[0], inc=1, device_id=(gx, lax.rem(gy + ngy + hop, ngy)), device_id_type=MESH)

    low_half = lane < 64

    def coarse_operands(c0, c1, top, bottom):
        swapped0, swapped1 = roll(c0, 64), roll(c1, 64)
        middle = jnp.where(low_half, swapped0, swapped1)
        before0 = jnp.where(low_half, top, swapped0)
        after1 = jnp.where(low_half, swapped1, bottom)
        def operand(p, q):
            h = halves(jnp.concatenate([p, q], axis=1))
            return jnp.concatenate([h, h], axis=0)
        return operand(c0, c1), operand(before0, middle), operand(middle, after1)

    def coarse_apply(c0, c1, top, bottom):
        here, before, after = coarse_operands(c0, c1, top, bottom)
        out = pick(dot(ct[0], here), ctb[0], csb[0])
        out = out + pick(dot(ct[1], before), ctb[1], csb[1])
        out = out + pick(dot(ct[2], after), ctb[2], csb[2])
        for d, shift in ((3, 1), (4, -1)):
            part = pick(dot(ct[d], here), ctb[d], csb[d])
            out = out + jnp.concatenate([roll(part[:, :128], shift), roll(part[:, 128:], shift)], axis=-1)
        return out

    def coarse_smooth(r):
        h = halves(r)
        return pick(dot(cs[...], jnp.concatenate([h, h], axis=0)), ctb[0], cc0)

    left_lanes = (lane == 127) | (lane == 63)
    right_lanes = (lane == 48) | (lane == 112)

    def background():
        copies = [
            send(rhs_s.at[pl.ds(TOP, 2)], ba_rhs_row.at[1], sb_sem.at[0], rb_sem.at[0], up),
            send(rhs_s.at[pl.ds(TOP + 6, 2)], ba_rhs_row.at[0], sb_sem.at[1], rb_sem.at[1], down),
            send(pack_mrow.at[0], ba_meta_row.at[1], sb_sem.at[2], rb_sem.at[2], up),
            send(pack_mrow.at[1], ba_meta_row.at[0], sb_sem.at[3], rb_sem.at[3], down),
        ]
        slot = 4
        for k, x in enumerate((gx, up[0], down[0])):
            for side, to in ((0, left[1]), (1, right[1])):
                copies.append(send(pack_mcol.at[side], ba_meta_col.at[k, side], sb_sem.at[slot], rb_sem.at[slot], (x, to)))
                copies.append(
                    send(pack_rhs.at[side], ba_rhs_col.at[k, side], sb_sem.at[slot + 1], rb_sem.at[slot + 1], (x, to))
                )
                slot += 2
        for k, to in enumerate((down, up, right, left)):
            copies.append(send(cpack, ba_cg.at[k], sb_sem.at[slot + k], rb_sem.at[slot + k], to))
        return copies

    def disseminate(level, hop):
        pl.semaphore_wait(dis.at[level], 2)
        if hop:
            for h in (hop, -hop):
                pl.semaphore_signal(
                    dis.at[level + 1], inc=1, device_id=(gx, lax.rem(gy + ngy + h, ngy)), device_id_type=MESH
                )

    def unpack_groups():
        lane1 = lanes_of((1, 128))
        is_left = (lane1 == 127) | (lane1 == 63)
        is_right = (lane1 == 48) | (lane1 == 112)
        codes = []
        for n in range(2):
            own = cpack[n:n + 1, :]
            code = jnp.where(own > 0.0, 8.0 * (own - 1.0), -1.0)
            fl = roll(ba_cg[2, n:n + 1, :], 80)
            fr = roll(ba_cg[3, n:n + 1, :], 48)
            code = jnp.where(is_left & has_left, 8.0 * (fl - 1.0) + 1.0, code)
            code = jnp.where(is_right & has_right, 8.0 * (fr - 1.0) + 2.0, code)
            codes.append(code)
        top = roll(ba_cg[0, 1:2, :], 64)
        bottom = roll(ba_cg[1, 0:1, :], 64)
        ends = jnp.full((1, 128), -1.0, F32)
        ends = jnp.where((lane1 < 48) & has_up, 8.0 * (top - 1.0) + 3.0, ends)
        ends = jnp.where((lane1 >= 64) & (lane1 < 112) & has_down, 8.0 * (bottom - 1.0) + 4.0, ends)
        codes.append(ends)
        rows = lax.broadcasted_iota(jnp.int32, (128, 128), 0)
        entry = jnp.where(rows < 32, lax.rem(rows, 16), 99).astype(F32)
        for n in range(3):
            hit = entry == jnp.broadcast_to(codes[n], (128, 128))
            onehot[:, 128 * n:128 * n + 128] = jnp.where(hit, 1.0, 0.0).astype(BF16)

    def unpack_halo():
        lane16 = lanes_of((16, 128))
        flags = ((has_left, has_right), (has_up, has_down))
        asm[...] = jnp.zeros_like(asm)
        for side in range(2):
            asm[side, 3:11, :] = ba_meta_col[0, side]
            asm[side, 1:3, :] = ba_meta_col[2, side, 6:8, :]
            asm[side, 11:13, :] = ba_meta_col[1, side, 0:2, :]
        for k in range(11):
            for rows, side, flag in ((slice(1, 3), 0, has_up), (slice(11, 13), 1, has_down)):
                block = ba_meta_row[side, 2 * k:2 * k + 2, :]
                meta[k, rows, :] = keep(flag, block) if k == 10 else block
            block = meta[k]
            fr = roll(asm[0], 96 - 2 * k)
            fl = roll(asm[1], 126 - 2 * k)
            if k == 10:
                fr, fl = keep(has_right, fr), keep(has_left, fl)
                row = lax.broadcasted_iota(jnp.int32, (16, 128), 0)
                dead = ((row < 3) & jnp.logical_not(has_up)) | ((row > 10) & jnp.logical_not(has_down))
                fr, fl = jnp.where(dead, 0.0, fr), jnp.where(dead, 0.0, fl)
            block = jnp.where((lane16 >= 96) & (lane16 < 98), fr, block)
            meta[k] = jnp.where(lane16 >= 126, fl, block)
        rhs_cols = [[unfold(ba_rhs_col[k, side]) for side in range(2)] for k in range(3)]
        for a in range(1, 13):
            if a < 3:
                block, source, i = ba_rhs_row[0, a - 1], 2, a + 5
            elif a < 11:
                block, source, i = rhs_s[a], 0, a - 3
            else:
                block, source, i = ba_rhs_row[1, a - 11], 1, a - 11
            rhs_s[a] = with_columns(block, rhs_cols[source][1], rhs_cols[source][0], i)
        weights(range(1, 13))

    behind = []
    e1_sent = []

    def taken(count, rows, sem):
        shape = rs_own.at[0, pl.ds(0, count), pl.ds(0, rows)]
        pltpu.make_async_copy(shape, shape, sem).wait()

    def correct(cycle):
        summed = jnp.zeros((128, 256), F32)
        for k in range(4):
            summed = summed + lax.dot_general(
                lv[k], member[:, 256 * k:256 * k + 256], (((1,), (1,)), ((), ())), preferred_element_type=F32
            )
        first_rhs = summed[:64] + summed[64:]
        fix = coarse_smooth(first_rhs)
        f0, f1 = fix[:, :128], fix[:, 128:]
        ff[cycle, 0] = f0
        ff[cycle, 1] = f1
        ff[cycle, 2] = jnp.where(
            (lane == 0) | (lane == 64), f0, jnp.where((lane == 1) | (lane == 65), roll(f1, 1), 0.0)
        )
        ff[cycle, 3] = jnp.where(
            (lane == 47) | (lane == 111), f0, jnp.where((lane == 48) | (lane == 112), roll(f1, 1), 0.0)
        )
        e1 = [
            send(ff.at[cycle, 0], e1_row.at[cycle, 1], s1.at[cycle, 0], r1.at[cycle, 1], up),
            send(ff.at[cycle, 1], e1_row.at[cycle, 0], s1.at[cycle, 1], r1.at[cycle, 0], down),
            send(ff.at[cycle, 2], e1_col.at[cycle, 1], s1.at[cycle, 2], r1.at[cycle, 3], left),
            send(ff.at[cycle, 3], e1_col.at[cycle, 0], s1.at[cycle, 3], r1.at[cycle, 2], right),
        ]
        e1_sent.extend(e1)
        if cycle == 0:
            behind.extend(background())
            disseminate(0, 4)
            disseminate(1, 1)
        for copy in e1:
            copy.wait_recv()
        top = roll(keep(has_up, e1_row[cycle, 0]), 64)
        bottom = roll(keep(has_down, e1_row[cycle, 1]), 64)
        fl = keep(has_left, e1_col[cycle, 0])
        fr = keep(has_right, e1_col[cycle, 1])
        h0 = jnp.where(left_lanes, roll(fl, 80), jnp.where(right_lanes, roll(fr, 48), f0))
        h1 = jnp.where(left_lanes, roll(fl, 79), jnp.where(right_lanes, roll(fr, 47), f1))
        leftover = first_rhs - coarse_apply(h0, h1, top, bottom)
        l0, l1 = leftover[:, :128], leftover[:, 128:]
        entries = []
        for h in range(2):
            m0 = jnp.broadcast_to(cpack[0:1, :] == h + 1.0, (64, 128))
            m1 = jnp.broadcast_to(cpack[1:2, :] == h + 1.0, (64, 128))
            total = jnp.where(m0, l0, 0.0) + jnp.where(m1, l1, 0.0)
            entries.append(jnp.sum(total, axis=1, keepdims=True))
        column = jnp.broadcast_to(jnp.concatenate(entries, axis=0), (128, 128))
        if cycle == 0:
            loads[12].wait()
        for q in range(ngy):
            row = jnp.sum(m_s[:, 128 * q:128 * q + 128] * column, axis=0, keepdims=True)
            parts[cycle, q, 0:1, :] = row
            if q + 1 < ngy:
                parts[cycle, q + 1, 1:2, :] = row
            if q > 0:
                parts[cycle, q - 1, 2:3, :] = row
        parts[cycle, 0, 1:2, :] = jnp.zeros((1, 128), F32)
        parts[cycle, ngy - 1, 2:3, :] = jnp.zeros((1, 128), F32)
        if cycle == 0:
            disseminate(2, 0)

        def own_copy(k):
            q = lax.rem(gy + k, ngy)
            return pltpu.make_async_remote_copy(
                src_ref=parts.at[cycle, q, pl.ds(0, 3)], dst_ref=rs_own.at[cycle, gy, pl.ds(0, 3)],
                send_sem=srs.at[cycle, 0], recv_sem=rrs.at[cycle], device_id=(gx, q), device_id_type=MESH,
            )

        def cross_copy(k, which):
            q = lax.rem(gy + k, ngy)
            to, dst = (up[0], rs_dn) if which == 0 else (down[0], rs_up)
            return pltpu.make_async_remote_copy(
                src_ref=parts.at[cycle, q, pl.ds(0, 1)], dst_ref=dst.at[cycle, gy, pl.ds(0, 1)],
                send_sem=srs.at[cycle, 1 + which], recv_sem=rrsx.at[cycle, which], device_id=(to, q), device_id_type=MESH,
            )

        for k in sorted(range(ngy), key=lambda k: -min(k, ngy - k)):
            if k > 0:
                own_copy(k).start()
            cross_copy(k, 0).start()
            cross_copy(k, 1).start()
        rs_own[cycle, gy, 0:3, :] = parts[cycle, gy, 0:3, :]
        if cycle == 0:
            for copy in behind:
                copy.wait()
            unpack_groups()
            unpack_halo()
        taken(ngy - 1, 3, rrs.at[cycle])
        taken(ngy, 1, rrsx.at[cycle, 0])
        taken(ngy, 1, rrsx.at[cycle, 1])
        own = rs_own[cycle, 0, 0:3, :]
        above = rs_up[cycle, 0, 0:1, :]
        below = rs_dn[cycle, 0, 0:1, :]
        for q in range(1, ngy):
            own = own + rs_own[cycle, q, 0:3, :]
            above = above + rs_up[cycle, q, 0:1, :]
            below = below + rs_dn[cycle, q, 0:1, :]
        five = jnp.concatenate([own, above, below, jnp.zeros((3, 128), F32)], axis=0)
        both_groups = jnp.concatenate([five, roll(five, 64)], axis=0)
        high = both_groups.astype(BF16).astype(F32)
        tall = jnp.concatenate([high, both_groups - high, jnp.zeros((96, 128), F32)], axis=0)
        lifted = dot(tall.T[0:64].astype(BF16), onehot[...])
        p0, p1, ends = lifted[:, :128], lifted[:, 128:256], lifted[:, 256:]
        rest = leftover - coarse_apply(p0, p1, ends, ends)
        fix = fix + lifted[:, :256] + coarse_smooth(rest)
        spread = dot(halves(fix), member[...])
        spread = spread[:64] + spread[64:]
        for i in range(8):
            block = spread[:, 128 * i:128 * i + 128].reshape(8, 8, 128) * fb[TOP + i][None]
            st[TOP + i] = st[TOP + i] + block.reshape(64, 128)

    def exchange(width, row_buf, col_buf, ssem, rsem, slot):
        pack_columns(st, slot, pack_st)
        copies = []
        n = 2
        for k, x in ((1, up[0]), (2, down[0])):
            for side, to in ((0, left[1]), (1, right[1])):
                copies.append(send(pack_st.at[slot + side], col_buf.at[k, side], ssem.at[n], rsem.at[n], (x, to)))
                n += 1
        copies.append(send(st.at[pl.ds(TOP, width)], row_buf.at[1], ssem.at[0], rsem.at[1], up))
        copies.append(send(st.at[pl.ds(TOP + 8 - width, width)], row_buf.at[0], ssem.at[1], rsem.at[0], down))
        for side, to in ((0, left), (1, right)):
            copies.append(send(pack_st.at[slot + side], col_buf.at[0, side], ssem.at[n], rsem.at[n], to))
            n += 1
        for copy in copies:
            copy.wait()
        cols = [
            [unfold(keep(flag, col_buf[k, side])) for side, flag in ((0, has_right), (1, has_left))] for k in range(3)
        ]
        for a in range(TOP - width, TOP + 8 + width):
            if a < 3:
                block, source, i, flag = row_buf[0, a - (TOP - width)], 2, a + 5, has_up
            elif a < 11:
                block, source, i, flag = st[a], 0, a - 3, None
            else:
                block, source, i, flag = row_buf[1, a - 11], 1, a - 11, has_down
            block = with_columns(block, cols[source][1], cols[source][0], i)
            if flag is not None:
                block = keep(flag, block)
            st[a] = block
            put(xa, a, block)

    level_rows(xa)
    for copy in e0:
        copy.wait_send()
    correct(0)
    exchange(3, e3_row, e3_col, s3, r3, 2)
    smooth_rows(xa, xb, 1, 6)
    smooth_rows(xb, xa, 2, 5)
    level_rows(xa)
    correct(1)
    exchange(2, e6_row, e6_col, s6, r6, 4)
    smooth_rows(xa, xb, 2, 5)

    def final_body(k, carry):
        a = TOP + 2 * k
        inside = jnp.concatenate([fb[a], fb[a + 1]], axis=-1)
        r = (both(rhs_s, a) - apply_pair(xb, a)).reshape(8, 8, 256) * inside[None]
        r = r.reshape(64, 256)
        for n in range(2):
            res_ref[2 * k + n] = r[:, 128 * n:128 * n + 96]
            sol_ref[2 * k + n] = st[a + n][:, 0:96]
        return carry

    lax.fori_loop(0, 4, final_body, 0, unroll=True)

    for copy in e1_sent:
        copy.wait_send()
    for cycle in range(2):
        taken(ngy - 1, 3, srs.at[cycle, 0])
        taken(ngy, 1, srs.at[cycle, 1])
        taken(ngy, 1, srs.at[cycle, 2])


def solution(mesh):
    ngx, ngy = mesh.shape["gx"], mesh.shape["gy"]

    def shards(
        rhs, active, fine_types, fine_scales, fine_table, fine_smoother, fine_groups,
        coarse_types, coarse_scales, coarse_table, coarse_smoother, coarse_groups, coarsest,
    ):
        vmem = pl.BlockSpec(memory_space=pltpu.VMEM)
        dma = pltpu.SemaphoreType.DMA
        sol, res = pl.pallas_call(
            functools.partial(kernel, ngx, ngy),
            out_shape=(pltpu.VMEM((8, 64, 96), F32),) * 2,
            in_specs=[pl.BlockSpec(memory_space=pltpu.HBM)] * 13,
            out_specs=(vmem, vmem),
            scratch_shapes=[
                pltpu.VMEM((8, 64, 96), F32),
                pltpu.VMEM((8, 96), jnp.int32),
                pltpu.VMEM((5, 8, 96), jnp.int32),
                pltpu.VMEM((5, 8, 96), F32),
                pltpu.VMEM((5, 4, 64, 64), F32),
                pltpu.VMEM((4, 64, 64), F32),
                pltpu.VMEM((8, 96), jnp.int32),
                pltpu.VMEM((5, 4, 48), jnp.int32),
                pltpu.VMEM((5, 4, 48), F32),
                pltpu.VMEM((5, 4, 64, 64), F32),
                pltpu.VMEM((4, 64, 64), F32),
                pltpu.VMEM((4, 48), jnp.int32),
                pltpu.VMEM((ROWS, 64, 128), F32),
                pltpu.VMEM((ROWS, 128, 128), BF16),
                pltpu.VMEM((ROWS, 128, 128), BF16),
                pltpu.VMEM((ROWS, 64, 128), F32),
                pltpu.VMEM((11, 16, 128), F32),
                pltpu.VMEM((8, 128), jnp.int32),
                pltpu.VMEM((5, ROWS, 8, 128), F32),
                pltpu.VMEM((5, ROWS, 8, 128), F32),
                pltpu.VMEM((ROWS, 8, 128), F32),
                pltpu.VMEM((ROWS, 8, 128), F32),
                pltpu.VMEM((11, 8, 128), F32),
                pltpu.VMEM((5, 8, 256), F32),
                pltpu.VMEM((5, 8, 256), F32),
                pltpu.VMEM((8, 256), F32),
                pltpu.VMEM((5, 256, 256), BF16),
                pltpu.VMEM((256, 256), BF16),
                pltpu.VMEM((5, 256, 256), BF16),
                pltpu.VMEM((256, 256), BF16),
                pltpu.VMEM((256, 1024), BF16),
                pltpu.VMEM((4, 128, 256), BF16),
                pltpu.VMEM((2, 4, 64, 128), F32),
                pltpu.VMEM((128, 128 * ngy), F32),
                pltpu.VMEM((2, 64, 128), F32),
                pltpu.VMEM((2, 16, 128), F32),
                pltpu.VMEM((2, 3, 64, 128), F32),
                pltpu.VMEM((3, 2, 16, 128), F32),
                pltpu.VMEM((2, 2, 64, 128), F32),
                pltpu.VMEM((3, 2, 16, 128), F32),
                pltpu.VMEM((2, 24, 128), F32),
                pltpu.VMEM((3, 2, 8, 128), F32),
                pltpu.VMEM((3, 2, 16, 128), F32),
                pltpu.VMEM((2, 2, 64, 128), F32),
                pltpu.VMEM((4, 8, 128), F32),
                pltpu.VMEM((2, 2, 64, 128), F32),
                pltpu.VMEM((2, 2, 64, 128), F32),
                pltpu.VMEM((2, ngy, 8, 128), F32),
                pltpu.VMEM((2, ngy, 8, 128), F32),
                pltpu.VMEM((2, ngy, 8, 128), F32),
                pltpu.VMEM((6, 16, 128), F32),
                pltpu.VMEM((2, 16, 128), F32),
                pltpu.VMEM((2, 24, 128), F32),
                pltpu.VMEM((2, 8, 128), F32),
                pltpu.VMEM((8, 128), F32),
                pltpu.VMEM((2, ngy, 8, 128), F32),
                pltpu.VMEM((2, 16, 128), F32),
                pltpu.VMEM((128, 384), BF16),
                dma((13,)),
                dma((4,)), dma((4,)),
                dma((20,)), dma((20,)),
                dma((2, 4)), dma((2, 4)),
                dma((2, 3)), dma((2,)), dma((2, 2)),
                dma((8,)), dma((8,)),
                dma((8,)), dma((8,)),
                pltpu.SemaphoreType.REGULAR((3,)),
            ],
            compiler_params=pltpu.CompilerParams(
                collective_id=0, has_side_effects=True, vmem_limit_bytes=60 * 2**20
            ),
        )(
            jnp.swapaxes(rhs, 1, 2), active, fine_types, fine_scales, fine_table, fine_smoother, fine_groups,
            coarse_types, coarse_scales, coarse_table, coarse_smoother, coarse_groups, coarsest,
        )
        return jnp.swapaxes(sol, 1, 2), jnp.swapaxes(res, 1, 2)

    return jax.shard_map(
        shards,
        mesh=mesh,
        in_specs=(
            P("gx", "gy", None),
            P("gx", "gy"),
            P(None, "gx", "gy"),
            P(None, "gx", "gy"),
            P(),
            P(),
            P("gx", "gy"),
            P(None, "gx", "gy"),
            P(None, "gx", "gy"),
            P(),
            P(),
            P("gx", "gy"),
            P("gx", "gy", None),
        ),
        out_specs=(P("gx", "gy", None), P("gx", "gy", None)),
        check_vma=False,
    )
```

```python
import functools

import jax
import jax.numpy as jnp
from jax import lax
from jax.experimental import pallas as pl
from jax.experimental.pallas import tpu as pltpu
from jax.sharding import PartitionSpec as P

MESH = pl.DeviceIdType.MESH
F32 = jnp.float32
BF16 = jnp.bfloat16
OMEGA = 0.7

TOP = 3
ROWS = 14


def lanes_of(shape):
    return lax.broadcasted_iota(jnp.int32, shape, len(shape) - 1)


def roll(x, shift):
    shift = shift % x.shape[-1]
    return x if shift == 0 else pltpu.roll(x, shift, x.ndim - 1)


def halves(x):
    high = x.astype(BF16)
    low = (x - high.astype(F32)).astype(BF16)
    return jnp.concatenate([high, low], axis=0)


def dot(a, b):
    return jnp.dot(a, b, preferred_element_type=F32)


def pick(products, kind, scale):
    width = products.shape[1]
    y = products.reshape(4, 8, 8, width)
    kind = jnp.broadcast_to(kind[None], (8, 8, width))
    out = jnp.where(kind == 1.0, y[1], y[0])
    out = jnp.where(kind == 2.0, y[2], out)
    out = jnp.where(kind == 3.0, y[3], out)
    return (out * scale[None]).reshape(64, width)


def kernel(
    ngx, ngy,
    rhs_in, active_in, ftypes_in, fscales_in, ftab_in, fsm_in, fgroups_in,
    ctypes_in, cscales_in, ctab_in, csm_in, cgroups_in, coarsest_in,
    sol_ref, res_ref,
    rhs_ref, active_ref, ftypes_ref, fscales_ref, ftab_ref, fsm_ref, fgroups_ref,
    ctypes_ref, cscales_ref, ctab_ref, csm_ref, cgroups_ref,
    st, xa, xb, rhs_s, meta, gplane, tb, sb, c0b, fb, cplane, ctb, csb, cc0,
    ft, fs, ct, cs, member, lv, ff, m_s,
    e0_row, e0_col, e3_row, e3_col, e6_row, e6_col, ba_meta_row, ba_meta_col, ba_rhs_col, ba_rhs_row, ba_cg,
    e1_row, e1_col, rs_own, rs_up, rs_dn,
    pack_st, pack_rhs, pack_mrow, pack_mcol, cpack, parts, asm, onehot,
    load_sem, s0, r0, sb_sem, rb_sem, s1, r1, srs, rrs, rrsx, s3, r3, s6, r6, dis,
):
    gx = lax.axis_index("gx")
    gy = lax.axis_index("gy")
    up = (lax.rem(gx + ngx - 1, ngx), gy)
    down = (lax.rem(gx + 1, ngx), gy)
    left = (gx, lax.rem(gy + ngy - 1, ngy))
    right = (gx, lax.rem(gy + 1, ngy))
    has_up, has_down = gx > 0, gx < ngx - 1
    has_left, has_right = gy > 0, gy < ngy - 1

    barrier = pltpu.get_barrier_semaphore()
    for to in (up, down, left, right):
        pl.semaphore_signal(barrier, inc=1, device_id=to, device_id_type=MESH)

    loads = [
        pltpu.make_async_copy(source, target, load_sem.at[n])
        for n, (source, target) in enumerate((
            (rhs_in, rhs_ref), (active_in, active_ref), (ftypes_in, ftypes_ref), (fscales_in, fscales_ref),
            (fsm_in, fsm_ref), (ftab_in, ftab_ref), (fgroups_in, fgroups_ref), (ctypes_in, ctypes_ref),
            (cscales_in, cscales_ref), (ctab_in, ctab_ref), (csm_in, csm_ref), (cgroups_in, cgroups_ref),
            (coarsest_in.at[0], m_s),
        ))
    ]
    for copy in loads:
        copy.start()

    def send(src, dst, ssem, rsem, to):
        copy = pltpu.make_async_remote_copy(
            src_ref=src, dst_ref=dst, send_sem=ssem, recv_sem=rsem, device_id=to, device_id_type=MESH
        )
        copy.start()
        return copy

    def keep(flag, x):
        return jnp.where(flag, x, jnp.zeros_like(x))

    lane = lanes_of((64, 128))

    st[...] = jnp.zeros_like(st)
    xa[...] = jnp.zeros_like(xa)
    xb[...] = jnp.zeros_like(xb)
    rhs_s[...] = jnp.zeros_like(rhs_s)
    meta[...] = jnp.zeros_like(meta)
    for copy in loads[:5]:
        copy.wait()
    for i in range(8):
        rhs_s[TOP + i, :, 0:96] = rhs_ref[i]
    for d in range(5):
        meta[d, TOP:TOP + 8, 0:96] = ftypes_ref[d].astype(F32)
        meta[5 + d, TOP:TOP + 8, 0:96] = fscales_ref[d]
    meta[10, TOP:TOP + 8, 0:96] = active_ref[...].astype(F32)
    def split_table(block):
        high = block.astype(BF16).astype(F32)
        low = block - high
        return jnp.concatenate([high, high, low, low], axis=1).astype(BF16)

    fs[...] = split_table(fsm_ref[...].reshape(256, 64))

    def weights(rows):
        for a in rows:
            for d in range(5):
                shift = {3: -1, 4: 1}.get(d, 0)
                tb[d, a] = jnp.broadcast_to(roll(meta[d, a:a + 1, :], shift), (8, 128))
                sb[d, a] = jnp.broadcast_to(roll(meta[5 + d, a:a + 1, :], shift), (8, 128))
            scale = meta[5, a:a + 1, :]
            inside = meta[10, a:a + 1, :]
            factor = jnp.where(scale > 0.0, OMEGA * inside / jnp.where(scale > 0.0, scale, 1.0), 0.0)
            c0b[a] = jnp.broadcast_to(factor, (8, 128))
            fb[a] = jnp.broadcast_to(inside, (8, 128))

    weights(range(TOP, TOP + 8))

    def both(ref, a):
        return jnp.concatenate([ref[a], ref[a + 1]], axis=-1)

    def rhs_operand(x, a):
        pair = both(x, a)
        return jnp.concatenate([pair, pair], axis=0)

    def apply_rows(x, first, pairs, consume):
        before = dot(ft[1024:1280], rhs_operand(x, first - 1))
        for k in range(pairs):
            a = first + 2 * k
            kinds = lambda d: jnp.concatenate([tb[d, a], tb[d, a + 1]], axis=-1)
            scales = lambda d: jnp.concatenate([sb[d, a], sb[d, a + 1]], axis=-1)
            here = dot(ft[0:768], rhs_operand(x, a))
            after = dot(ft[768:1024] if k == pairs - 1 else ft[768:1280], rhs_operand(x, a + 1))
            out = pick(here[0:256], kinds(0), scales(0))
            out = out + pick(before, kinds(1), scales(1))
            out = out + pick(after[0:256], kinds(2), scales(2))
            for d, shift in ((3, 1), (4, -1)):
                part = pick(here[256 * (d - 2):256 * (d - 1)], kinds(d), scales(d))
                out = out + jnp.concatenate([roll(part[:, :128], shift), roll(part[:, 128:], shift)], axis=-1)
            before = after[256:]
            consume(a, out)

    def smooth_pair(r, a):
        parts2 = halves(r)
        y = dot(fs[...], jnp.concatenate([parts2, parts2], axis=0))
        kind = jnp.concatenate([tb[0, a], tb[0, a + 1]], axis=-1)
        factor = jnp.concatenate([c0b[a], c0b[a + 1]], axis=-1)
        return pick(y, kind, factor)

    def put(x, a, value):
        x[a] = halves(value)

    def smooth_rows(source, target, first, pairs):
        def consume(a, out):
            r = both(rhs_s, a) - out
            new = both(st, a) + smooth_pair(r, a)
            for n in range(2):
                part = new[:, 128 * n:128 * n + 128]
                st[a + n] = part
                put(target, a + n, part)

        apply_rows(source, first, pairs, consume)

    def level_rows(source, first, pairs):
        def consume(a, out):
            inside = jnp.concatenate([fb[a], fb[a + 1]], axis=-1)
            r = (both(rhs_s, a) - out).reshape(8, 8, 256) * inside[None]
            lv[(a - TOP) // 2] = halves(r.reshape(64, 256))

        apply_rows(source, first, pairs, consume)

    def first_body(k, carry):
        a = TOP + 2 * k
        new = smooth_pair(both(rhs_s, a), a)
        for n in range(2):
            part = new[:, 128 * n:128 * n + 128]
            st[a + n] = part
            put(xa, a + n, part)
        return carry

    lax.fori_loop(0, 4, first_body, 0, unroll=True)

    def pack_columns(field, slot, out):
        first = jnp.zeros((64, 128), F32)
        last = jnp.zeros((64, 128), F32)
        for i in range(8):
            block = field[TOP + i]
            mask = (lane >= 4 * i) & (lane < 4 * i + 3)
            first = jnp.where(mask, roll(block, 4 * i), first)
            last = jnp.where(mask, roll(block, 4 * i - 93), last)
        for n, block in ((0, first), (1, last)):
            out[slot + n] = sum(roll(block[16 * m:16 * m + 16], 32 * m) for m in range(4))

    def unfold(block):
        return jnp.concatenate([roll(block, -32 * m) for m in range(4)], axis=0)

    def with_columns(block, from_left, from_right, i):
        block = jnp.where((lane >= 96) & (lane < 99), roll(from_right, 96 - 4 * i), block)
        return jnp.where(lane >= 125, roll(from_left, 125 - 4 * i), block)

    pack_columns(st, 0, pack_st)
    pl.semaphore_wait(barrier, 4)
    e0 = [
        send(st.at[TOP], e0_row.at[1], s0.at[0], r0.at[1], up),
        send(st.at[TOP + 7], e0_row.at[0], s0.at[1], r0.at[0], down),
        send(pack_st.at[0], e0_col.at[1], s0.at[2], r0.at[3], left),
        send(pack_st.at[1], e0_col.at[0], s0.at[3], r0.at[2], right),
    ]

    for copy in loads[5:12]:
        copy.wait()
    cplane[...] = jnp.zeros_like(cplane)
    gplane[...] = jnp.full_like(gplane, -1)
    for d in range(5):
        cplane[d, 0:4, 0:48] = ctypes_ref[d].astype(F32)
        cplane[5 + d, 0:4, 0:48] = cscales_ref[d]
        place = 256 * (0, 4, 3, 1, 2)[d]
        ft[place:place + 256] = split_table(ftab_ref[d].reshape(256, 64))
        ct[place:place + 256] = split_table(ctab_ref[d].reshape(256, 64))
    cs[...] = split_table(csm_ref[...].reshape(256, 64))
    g = fgroups_ref[...]
    step = lambda k: (g >= 48 * k).astype(jnp.int32)
    gplane[0:8, 0:96] = g + 16 * (step(1) + step(2) + step(3))
    cplane[10, 0:4, 0:48] = (cgroups_ref[...] + 1).astype(F32)
    row256 = lax.broadcasted_iota(jnp.int32, (256, 128), 0)
    for i in range(8):
        code = jnp.broadcast_to(gplane[i:i + 1, :], (256, 128))
        member[:, 128 * i:128 * i + 128] = jnp.where(row256 == code, 1.0, 0.0).astype(BF16)

    cweights = []
    for k in range(11):
        plane = cplane[k]
        low = plane[0:1, :] + roll(plane[1:2, :], 64)
        high = plane[2:3, :] + roll(plane[3:4, :], 64)
        cweights.append((low, high))
    for d in range(5):
        shift = {3: -1, 4: 1}.get(d, 0)
        for n in range(2):
            ctb[d, :, 128 * n:128 * n + 128] = jnp.broadcast_to(roll(cweights[d][n], shift), (8, 128))
            csb[d, :, 128 * n:128 * n + 128] = jnp.broadcast_to(roll(cweights[5 + d][n], shift), (8, 128))
    for n in range(2):
        scale = cweights[5][n]
        factor = jnp.where(scale > 0.0, OMEGA / jnp.where(scale > 0.0, scale, 1.0), 0.0)
        cc0[:, 128 * n:128 * n + 128] = jnp.broadcast_to(factor, (8, 128))
    cpack[...] = jnp.concatenate([cweights[10][0], cweights[10][1], jnp.zeros((6, 128), F32)], axis=0)

    for k in range(11):
        pack_mrow[0, 2 * k:2 * k + 2, :] = meta[k, TOP:TOP + 2, :]
        pack_mrow[1, 2 * k:2 * k + 2, :] = meta[k, TOP + 6:TOP + 8, :]
    pack_mrow[0, 22:24, :] = jnp.zeros((2, 128), F32)
    pack_mrow[1, 22:24, :] = jnp.zeros((2, 128), F32)
    lane8 = lanes_of((8, 128))
    first = jnp.zeros((8, 128), F32)
    last = jnp.zeros((8, 128), F32)
    for k in range(11):
        block = meta[k, TOP:TOP + 8, :]
        mask = (lane8 >= 2 * k) & (lane8 < 2 * k + 2)
        first = jnp.where(mask, roll(block, 2 * k), first)
        last = jnp.where(mask, roll(block, 2 * k - 94), last)
    pack_mcol[0] = first
    pack_mcol[1] = last
    pack_columns(rhs_s, 0, pack_rhs)

    for copy in e0[2:]:
        copy.wait_recv()
    from_left = unfold(keep(has_left, e0_col[0]))
    from_right = unfold(keep(has_right, e0_col[1]))
    for i in range(8):
        put(xa, TOP + i, with_columns(st[TOP + i], from_left, from_right, i))
    level_rows(xa, TOP + 2, 2)
    for copy in e0[:2]:
        copy.wait_recv()
    put(xa, TOP - 1, keep(has_up, e0_row[0]))
    put(xa, TOP + 8, keep(has_down, e0_row[1]))
    for k, hop in enumerate((2, -2)):
        pl.semaphore_signal(dis.at[0], inc=1, device_id=(gx, lax.rem(gy + ngy + hop, ngy)), device_id_type=MESH)

    low_half = lane < 64

    def coarse_operands(c0, c1, top, bottom):
        swapped0, swapped1 = roll(c0, 64), roll(c1, 64)
        middle = jnp.where(low_half, swapped0, swapped1)
        before0 = jnp.where(low_half, top, swapped0)
        after1 = jnp.where(low_half, swapped1, bottom)
        def operand(p, q):
            h = halves(jnp.concatenate([p, q], axis=1))
            return jnp.concatenate([h, h], axis=0)
        return operand(c0, c1), operand(before0, middle), operand(middle, after1)

    def coarse_apply(c0, c1, top, bottom):
        here, before, after = coarse_operands(c0, c1, top, bottom)
        y = dot(ct[0:768], here)
        out = pick(y[0:256], ctb[0], csb[0])
        out = out + pick(dot(ct[1024:1280], before), ctb[1], csb[1])
        out = out + pick(dot(ct[768:1024], after), ctb[2], csb[2])
        for d, shift in ((3, 1), (4, -1)):
            part = pick(y[256 * (d - 2):256 * (d - 1)], ctb[d], csb[d])
            out = out + jnp.concatenate([roll(part[:, :128], shift), roll(part[:, 128:], shift)], axis=-1)
        return out

    def coarse_smooth(r):
        h = halves(r)
        return pick(dot(cs[...], jnp.concatenate([h, h], axis=0)), ctb[0], cc0)

    left_lanes = (lane == 127) | (lane == 63)
    right_lanes = (lane == 48) | (lane == 112)

    def background():
        copies = [
            send(rhs_s.at[pl.ds(TOP, 2)], ba_rhs_row.at[1], sb_sem.at[0], rb_sem.at[0], up),
            send(rhs_s.at[pl.ds(TOP + 6, 2)], ba_rhs_row.at[0], sb_sem.at[1], rb_sem.at[1], down),
            send(pack_mrow.at[0], ba_meta_row.at[1], sb_sem.at[2], rb_sem.at[2], up),
            send(pack_mrow.at[1], ba_meta_row.at[0], sb_sem.at[3], rb_sem.at[3], down),
        ]
        slot = 4
        for k, x in enumerate((gx, up[0], down[0])):
            for side, to in ((0, left[1]), (1, right[1])):
                copies.append(send(pack_mcol.at[side], ba_meta_col.at[k, side], sb_sem.at[slot], rb_sem.at[slot], (x, to)))
                copies.append(
                    send(pack_rhs.at[side], ba_rhs_col.at[k, side], sb_sem.at[slot + 1], rb_sem.at[slot + 1], (x, to))
                )
                slot += 2
        for k, to in enumerate((down, up, right, left)):
            copies.append(send(cpack, ba_cg.at[k], sb_sem.at[slot + k], rb_sem.at[slot + k], to))
        return copies

    def disseminate(level, hop):
        pl.semaphore_wait(dis.at[level], 2)
        if hop:
            for h in (hop, -hop):
                pl.semaphore_signal(
                    dis.at[level + 1], inc=1, device_id=(gx, lax.rem(gy + ngy + h, ngy)), device_id_type=MESH
                )

    def unpack_groups():
        lane1 = lanes_of((1, 128))
        is_left = (lane1 == 127) | (lane1 == 63)
        is_right = (lane1 == 48) | (lane1 == 112)
        codes = []
        for n in range(2):
            own = cpack[n:n + 1, :]
            code = jnp.where(own > 0.0, 8.0 * (own - 1.0), -1.0)
            fl = roll(ba_cg[2, n:n + 1, :], 80)
            fr = roll(ba_cg[3, n:n + 1, :], 48)
            code = jnp.where(is_left & has_left, 8.0 * (fl - 1.0) + 1.0, code)
            code = jnp.where(is_right & has_right, 8.0 * (fr - 1.0) + 2.0, code)
            codes.append(code)
        top = roll(ba_cg[0, 1:2, :], 64)
        bottom = roll(ba_cg[1, 0:1, :], 64)
        ends = jnp.full((1, 128), -1.0, F32)
        ends = jnp.where((lane1 < 48) & has_up, 8.0 * (top - 1.0) + 3.0, ends)
        ends = jnp.where((lane1 >= 64) & (lane1 < 112) & has_down, 8.0 * (bottom - 1.0) + 4.0, ends)
        codes.append(ends)
        rows = lax.broadcasted_iota(jnp.int32, (128, 128), 0)
        entry = jnp.where(rows < 32, lax.rem(rows, 16), 99).astype(F32)
        for n in range(3):
            hit = entry == jnp.broadcast_to(codes[n], (128, 128))
            onehot[:, 128 * n:128 * n + 128] = jnp.where(hit, 1.0, 0.0).astype(BF16)

    def unpack_halo():
        lane16 = lanes_of((16, 128))
        flags = ((has_left, has_right), (has_up, has_down))
        asm[...] = jnp.zeros_like(asm)
        for side in range(2):
            asm[side, 3:11, :] = ba_meta_col[0, side]
            asm[side, 1:3, :] = ba_meta_col[2, side, 6:8, :]
            asm[side, 11:13, :] = ba_meta_col[1, side, 0:2, :]
        for k in range(11):
            for rows, side, flag in ((slice(1, 3), 0, has_up), (slice(11, 13), 1, has_down)):
                block = ba_meta_row[side, 2 * k:2 * k + 2, :]
                meta[k, rows, :] = keep(flag, block) if k == 10 else block
            block = meta[k]
            fr = roll(asm[0], 96 - 2 * k)
            fl = roll(asm[1], 126 - 2 * k)
            if k == 10:
                fr, fl = keep(has_right, fr), keep(has_left, fl)
                row = lax.broadcasted_iota(jnp.int32, (16, 128), 0)
                dead = ((row < 3) & jnp.logical_not(has_up)) | ((row > 10) & jnp.logical_not(has_down))
                fr, fl = jnp.where(dead, 0.0, fr), jnp.where(dead, 0.0, fl)
            block = jnp.where((lane16 >= 96) & (lane16 < 98), fr, block)
            meta[k] = jnp.where(lane16 >= 126, fl, block)
        rhs_cols = [[unfold(ba_rhs_col[k, side]) for side in range(2)] for k in range(3)]
        for a in range(1, 13):
            if a < 3:
                block, source, i = ba_rhs_row[0, a - 1], 2, a + 5
            elif a < 11:
                block, source, i = rhs_s[a], 0, a - 3
            else:
                block, source, i = ba_rhs_row[1, a - 11], 1, a - 11
            rhs_s[a] = with_columns(block, rhs_cols[source][1], rhs_cols[source][0], i)
        weights(range(1, 13))

    behind = []
    e1_sent = []

    def taken(count, rows, sem):
        shape = rs_own.at[0, pl.ds(0, count), pl.ds(0, rows)]
        pltpu.make_async_copy(shape, shape, sem).wait()

    def correct(cycle):
        summed = jnp.zeros((128, 256), F32)
        for k in range(4):
            summed = summed + lax.dot_general(
                lv[k], member[:, 256 * k:256 * k + 256], (((1,), (1,)), ((), ())), preferred_element_type=F32
            )
        first_rhs = summed[:64] + summed[64:]
        fix = coarse_smooth(first_rhs)
        f0, f1 = fix[:, :128], fix[:, 128:]
        ff[cycle, 0] = f0
        ff[cycle, 1] = f1
        ff[cycle, 2] = jnp.where(
            (lane == 0) | (lane == 64), f0, jnp.where((lane == 1) | (lane == 65), roll(f1, 1), 0.0)
        )
        ff[cycle, 3] = jnp.where(
            (lane == 47) | (lane == 111), f0, jnp.where((lane == 48) | (lane == 112), roll(f1, 1), 0.0)
        )
        e1 = [
            send(ff.at[cycle, 0], e1_row.at[cycle, 1], s1.at[cycle, 0], r1.at[cycle, 1], up),
            send(ff.at[cycle, 1], e1_row.at[cycle, 0], s1.at[cycle, 1], r1.at[cycle, 0], down),
            send(ff.at[cycle, 2], e1_col.at[cycle, 1], s1.at[cycle, 2], r1.at[cycle, 3], left),
            send(ff.at[cycle, 3], e1_col.at[cycle, 0], s1.at[cycle, 3], r1.at[cycle, 2], right),
        ]
        e1_sent.extend(e1)
        if cycle == 0:
            behind.extend(background())
            disseminate(0, 4)
            disseminate(1, 1)
        for copy in e1:
            copy.wait_recv()
        top = roll(keep(has_up, e1_row[cycle, 0]), 64)
        bottom = roll(keep(has_down, e1_row[cycle, 1]), 64)
        fl = keep(has_left, e1_col[cycle, 0])
        fr = keep(has_right, e1_col[cycle, 1])
        h0 = jnp.where(left_lanes, roll(fl, 80), jnp.where(right_lanes, roll(fr, 48), f0))
        h1 = jnp.where(left_lanes, roll(fl, 79), jnp.where(right_lanes, roll(fr, 47), f1))
        leftover = first_rhs - coarse_apply(h0, h1, top, bottom)
        l0, l1 = leftover[:, :128], leftover[:, 128:]
        entries = []
        for h in range(2):
            m0 = jnp.broadcast_to(cpack[0:1, :] == h + 1.0, (64, 128))
            m1 = jnp.broadcast_to(cpack[1:2, :] == h + 1.0, (64, 128))
            total = jnp.where(m0, l0, 0.0) + jnp.where(m1, l1, 0.0)
            entries.append(jnp.sum(total, axis=1, keepdims=True))
        column = jnp.broadcast_to(jnp.concatenate(entries, axis=0), (128, 128))
        if cycle == 0:
            loads[12].wait()
        for q in range(ngy):
            row = jnp.sum(m_s[:, 128 * q:128 * q + 128] * column, axis=0, keepdims=True)
            parts[cycle, q, 0:1, :] = row
            if q + 1 < ngy:
                parts[cycle, q + 1, 1:2, :] = row
            if q > 0:
                parts[cycle, q - 1, 2:3, :] = row
        parts[cycle, 0, 1:2, :] = jnp.zeros((1, 128), F32)
        parts[cycle, ngy - 1, 2:3, :] = jnp.zeros((1, 128), F32)
        if cycle == 0:
            disseminate(2, 0)

        def own_copy(k):
            q = lax.rem(gy + k, ngy)
            return pltpu.make_async_remote_copy(
                src_ref=parts.at[cycle, q, pl.ds(0, 3)], dst_ref=rs_own.at[cycle, gy, pl.ds(0, 3)],
                send_sem=srs.at[cycle, 0], recv_sem=rrs.at[cycle], device_id=(gx, q), device_id_type=MESH,
            )

        def cross_copy(k, which):
            q = lax.rem(gy + k, ngy)
            to, dst = (up[0], rs_dn) if which == 0 else (down[0], rs_up)
            return pltpu.make_async_remote_copy(
                src_ref=parts.at[cycle, q, pl.ds(0, 1)], dst_ref=dst.at[cycle, gy, pl.ds(0, 1)],
                send_sem=srs.at[cycle, 1 + which], recv_sem=rrsx.at[cycle, which], device_id=(to, q), device_id_type=MESH,
            )

        for k in sorted(range(ngy), key=lambda k: -min(k, ngy - k)):
            if k > 0:
                own_copy(k).start()
            cross_copy(k, 0).start()
            cross_copy(k, 1).start()
        rs_own[cycle, gy, 0:3, :] = parts[cycle, gy, 0:3, :]
        if cycle == 0:
            for copy in behind:
                copy.wait()
            unpack_groups()
            unpack_halo()
        taken(ngy - 1, 3, rrs.at[cycle])
        taken(ngy, 1, rrsx.at[cycle, 0])
        taken(ngy, 1, rrsx.at[cycle, 1])
        own = rs_own[cycle, 0, 0:3, :]
        above = rs_up[cycle, 0, 0:1, :]
        below = rs_dn[cycle, 0, 0:1, :]
        for q in range(1, ngy):
            own = own + rs_own[cycle, q, 0:3, :]
            above = above + rs_up[cycle, q, 0:1, :]
            below = below + rs_dn[cycle, q, 0:1, :]
        five = jnp.concatenate([own, above, below, jnp.zeros((3, 128), F32)], axis=0)
        both_groups = jnp.concatenate([five, roll(five, 64)], axis=0)
        high = both_groups.astype(BF16).astype(F32)
        tall = jnp.concatenate([high, both_groups - high, jnp.zeros((96, 128), F32)], axis=0)
        lifted = dot(tall.T[0:64].astype(BF16), onehot[...])
        p0, p1, ends = lifted[:, :128], lifted[:, 128:256], lifted[:, 256:]
        rest = leftover - coarse_apply(p0, p1, ends, ends)
        fix = fix + lifted[:, :256] + coarse_smooth(rest)
        spread = dot(halves(fix), member[...])
        spread = spread[:64] + spread[64:]
        for i in range(8):
            block = spread[:, 128 * i:128 * i + 128].reshape(8, 8, 128) * fb[TOP + i][None]
            st[TOP + i] = st[TOP + i] + block.reshape(64, 128)

    def exchange(width, row_buf, col_buf, ssem, rsem, slot, middle):
        pack_columns(st, slot, pack_st)
        copies = []
        n = 2
        for k, x in ((1, up[0]), (2, down[0])):
            for side, to in ((0, left[1]), (1, right[1])):
                copies.append(send(pack_st.at[slot + side], col_buf.at[k, side], ssem.at[n], rsem.at[n], (x, to)))
                n += 1
        copies.append(send(st.at[pl.ds(TOP, width)], row_buf.at[1], ssem.at[0], rsem.at[1], up))
        copies.append(send(st.at[pl.ds(TOP + 8 - width, width)], row_buf.at[0], ssem.at[1], rsem.at[0], down))
        for side, to in ((0, left), (1, right)):
            copies.append(send(pack_st.at[slot + side], col_buf.at[0, side], ssem.at[n], rsem.at[n], to))
            n += 1
        far, near = copies[:-2], copies[-2:]

        def columns(k):
            return [unfold(keep(flag, col_buf[k, side])) for side, flag in ((0, has_right), (1, has_left))]

        for copy in near:
            copy.wait()
        for copy in far:
            copy.wait_send()
        beside = columns(0)
        for i in range(8):
            block = with_columns(st[TOP + i], beside[1], beside[0], i)
            st[TOP + i] = block
            put(xa, TOP + i, block)
        middle()
        for copy in far:
            copy.wait_recv()
        above, below = columns(2), columns(1)
        for n in range(width):
            a = TOP - width + n
            block = keep(has_up, with_columns(row_buf[0, n], above[1], above[0], a + 5))
            st[a] = block
            put(xa, a, block)
            block = keep(has_down, with_columns(row_buf[1, n], below[1], below[0], n))
            st[TOP + 8 + n] = block
            put(xa, TOP + 8 + n, block)

    level_rows(xa, TOP, 1)
    level_rows(xa, TOP + 6, 1)
    for copy in e0:
        copy.wait_send()
    correct(0)
    exchange(3, e3_row, e3_col, s3, r3, 2, lambda: smooth_rows(xa, xb, 5, 2))
    smooth_rows(xa, xb, 1, 2)
    smooth_rows(xa, xb, 9, 2)
    smooth_rows(xb, xa, 2, 5)
    level_rows(xa, TOP, 4)
    correct(1)
    exchange(2, e6_row, e6_col, s6, r6, 4, lambda: smooth_rows(xa, xb, 4, 3))
    smooth_rows(xa, xb, 2, 1)
    smooth_rows(xa, xb, 10, 1)

    def final_pair(a, out):
        inside = jnp.concatenate([fb[a], fb[a + 1]], axis=-1)
        r = ((both(rhs_s, a) - out).reshape(8, 8, 256) * inside[None]).reshape(64, 256)
        for n in range(2):
            res_ref[a - TOP + n] = r[:, 128 * n:128 * n + 96]
            sol_ref[a - TOP + n] = st[a + n][:, 0:96]

    apply_rows(xb, TOP, 4, final_pair)

    for copy in e1_sent:
        copy.wait_send()
    for cycle in range(2):
        taken(ngy - 1, 3, srs.at[cycle, 0])
        taken(ngy, 1, srs.at[cycle, 1])
        taken(ngy, 1, srs.at[cycle, 2])


def solution(mesh):
    ngx, ngy = mesh.shape["gx"], mesh.shape["gy"]

    def shards(
        rhs, active, fine_types, fine_scales, fine_table, fine_smoother, fine_groups,
        coarse_types, coarse_scales, coarse_table, coarse_smoother, coarse_groups, coarsest,
    ):
        vmem = pl.BlockSpec(memory_space=pltpu.VMEM)
        dma = pltpu.SemaphoreType.DMA
        sol, res = pl.pallas_call(
            functools.partial(kernel, ngx, ngy),
            out_shape=(pltpu.VMEM((8, 64, 96), F32),) * 2,
            in_specs=[pl.BlockSpec(memory_space=pltpu.HBM)] * 13,
            out_specs=(vmem, vmem),
            scratch_shapes=[
                pltpu.VMEM((8, 64, 96), F32),
                pltpu.VMEM((8, 96), jnp.int32),
                pltpu.VMEM((5, 8, 96), jnp.int32),
                pltpu.VMEM((5, 8, 96), F32),
                pltpu.VMEM((5, 4, 64, 64), F32),
                pltpu.VMEM((4, 64, 64), F32),
                pltpu.VMEM((8, 96), jnp.int32),
                pltpu.VMEM((5, 4, 48), jnp.int32),
                pltpu.VMEM((5, 4, 48), F32),
                pltpu.VMEM((5, 4, 64, 64), F32),
                pltpu.VMEM((4, 64, 64), F32),
                pltpu.VMEM((4, 48), jnp.int32),
                pltpu.VMEM((ROWS, 64, 128), F32),
                pltpu.VMEM((ROWS, 128, 128), BF16),
                pltpu.VMEM((ROWS, 128, 128), BF16),
                pltpu.VMEM((ROWS, 64, 128), F32),
                pltpu.VMEM((11, 16, 128), F32),
                pltpu.VMEM((8, 128), jnp.int32),
                pltpu.VMEM((5, ROWS, 8, 128), F32),
                pltpu.VMEM((5, ROWS, 8, 128), F32),
                pltpu.VMEM((ROWS, 8, 128), F32),
                pltpu.VMEM((ROWS, 8, 128), F32),
                pltpu.VMEM((11, 8, 128), F32),
                pltpu.VMEM((5, 8, 256), F32),
                pltpu.VMEM((5, 8, 256), F32),
                pltpu.VMEM((8, 256), F32),
                pltpu.VMEM((1280, 256), BF16),
                pltpu.VMEM((256, 256), BF16),
                pltpu.VMEM((1280, 256), BF16),
                pltpu.VMEM((256, 256), BF16),
                pltpu.VMEM((256, 1024), BF16),
                pltpu.VMEM((4, 128, 256), BF16),
                pltpu.VMEM((2, 4, 64, 128), F32),
                pltpu.VMEM((128, 128 * ngy), F32),
                pltpu.VMEM((2, 64, 128), F32),
                pltpu.VMEM((2, 16, 128), F32),
                pltpu.VMEM((2, 3, 64, 128), F32),
                pltpu.VMEM((3, 2, 16, 128), F32),
                pltpu.VMEM((2, 2, 64, 128), F32),
                pltpu.VMEM((3, 2, 16, 128), F32),
                pltpu.VMEM((2, 24, 128), F32),
                pltpu.VMEM((3, 2, 8, 128), F32),
                pltpu.VMEM((3, 2, 16, 128), F32),
                pltpu.VMEM((2, 2, 64, 128), F32),
                pltpu.VMEM((4, 8, 128), F32),
                pltpu.VMEM((2, 2, 64, 128), F32),
                pltpu.VMEM((2, 2, 64, 128), F32),
                pltpu.VMEM((2, ngy, 8, 128), F32),
                pltpu.VMEM((2, ngy, 8, 128), F32),
                pltpu.VMEM((2, ngy, 8, 128), F32),
                pltpu.VMEM((6, 16, 128), F32),
                pltpu.VMEM((2, 16, 128), F32),
                pltpu.VMEM((2, 24, 128), F32),
                pltpu.VMEM((2, 8, 128), F32),
                pltpu.VMEM((8, 128), F32),
                pltpu.VMEM((2, ngy, 8, 128), F32),
                pltpu.VMEM((2, 16, 128), F32),
                pltpu.VMEM((128, 384), BF16),
                dma((13,)),
                dma((4,)), dma((4,)),
                dma((20,)), dma((20,)),
                dma((2, 4)), dma((2, 4)),
                dma((2, 3)), dma((2,)), dma((2, 2)),
                dma((8,)), dma((8,)),
                dma((8,)), dma((8,)),
                pltpu.SemaphoreType.REGULAR((3,)),
            ],
            compiler_params=pltpu.CompilerParams(
                collective_id=0, has_side_effects=True, vmem_limit_bytes=60 * 2**20
            ),
        )(
            jnp.swapaxes(rhs, 1, 2), active, fine_types, fine_scales, fine_table, fine_smoother, fine_groups,
            coarse_types, coarse_scales, coarse_table, coarse_smoother, coarse_groups, coarsest,
        )
        return jnp.swapaxes(sol, 1, 2), jnp.swapaxes(res, 1, 2)

    return jax.shard_map(
        shards,
        mesh=mesh,
        in_specs=(
            P("gx", "gy", None),
            P("gx", "gy"),
            P(None, "gx", "gy"),
            P(None, "gx", "gy"),
            P(),
            P(),
            P("gx", "gy"),
            P(None, "gx", "gy"),
            P(None, "gx", "gy"),
            P(),
            P(),
            P("gx", "gy"),
            P("gx", "gy", None),
        ),
        out_specs=(P("gx", "gy", None), P("gx", "gy", None)),
        check_vma=False,
    )
```
